256 devices in a mesh: leaf: 64 (over y, x, z_hi), probe: 4 (over z_lo, core).
Axes of the slice: x: 4, y: 4, z: 8 (z_hi: 4, z_lo: 2; z = z_hi * 2 + z_lo), core: 2. Of those that a mesh axis runs over, the one named last changes fastest.
Arguments:
- leaf_blocks: float32 [65536, 1024], P('leaf'), may hold values from -0.1875 to 0.1875
- block_mask: int32 [64, 8, 8], P('leaf'), may hold values 0 or 1
- row_factor_stack: float32 [6, 65536, 128], P(None, 'leaf'), may hold values from -0.5 to 0.5
- column_factor_stack: float32 [6, 65536, 128], P(None, 'leaf'), may hold values from -0.0234375 to 0.0234375
- probes: float32 [65536, 1024], P('leaf', 'probe'), may hold values from -6 to 6
Outputs:
- applied: float32 [65536, 1024], P('leaf', 'probe')
- probe_gram: float32 [1024, 1024], P('leaf', 'probe')
The draws below stay inside these ranges and needn't reach their ends.
All inputs are finite; a program needn't handle non-finite values. No bound on the sum of `block_mask` on one device may be relied on, other than what follows from the above.
Results may differ from the reference program's by a relative error of at most 0.0001.
Values sent between devices are 32-bit elements; how exact they have to be, the bound alone decides.
No kernel may reach another device: no remote copies, remote signals or barrier semaphores. Data moves between devices by JAX's collectives and lax.ppermute only.
A program may use at most 64 MiB of HBM per device.

```python
import jax
import jax.numpy as jnp
from jax import lax

LEAF_PTS = 1024
MB = 8
RANK = 128
PROBES = 1024
LEVELS = 6
POINTS = 65536
N_LEAF = 64


def touch_ends(drawn, key, smallest, high):
    longest = drawn.shape.index(max(drawn.shape))
    spots = []
    for shift in (0, 1):
        where = [jax.random.randint(jax.random.fold_in(key, axis), (), 0, length) for axis, length in enumerate(drawn.shape)]
        where[longest] = (where[longest] + shift) % drawn.shape[longest]
        spots.append(tuple(where))
    return drawn.at[spots[0]].set(smallest).at[spots[1]].set(high)


def block_scale(key, dims, shards, least, largest):
    loudness, own = 1.0, jax.random.fold_in(key, 6)
    for dim, blocks in shards:
        steps = jnp.exp(jax.random.uniform(jax.random.fold_in(own, dim), (blocks,), jnp.float32, least / len(shards), largest / len(shards)))
        loudness = loudness * jnp.repeat(steps, dims[dim] // blocks).reshape([-1 if axis == dim else 1 for axis in range(len(dims))])
    return loudness


def normal_values(key, dims, deviation, bound, cuts=(), kind=jnp.bfloat16):
    values = jax.random.normal(key, dims, jnp.float32) * deviation
    if len(cuts) > 0:
        values = block_scale(key, dims, cuts, -0.22, 0.18) * values
    return jnp.clip(values, min=-bound, max=bound).astype(kind)


def setup_inputs(seed: int = 0) -> dict:
    keys = jax.random.split(jax.random.key(seed), 6)
    leaf_blocks = normal_values(keys[0], (POINTS, LEAF_PTS), LEAF_PTS ** -0.5, 0.1875, ((0, 64),), jnp.float32)
    block_mask = touch_ends((jax.random.randint(keys[1], (N_LEAF, MB, MB), 0, 4) < 3).astype(jnp.int32), jax.random.fold_in(keys[1], 1), 0, 1)
    row_factor_stack = normal_values(keys[2], (LEVELS, POINTS, RANK), RANK ** -0.5, 0.5, ((1, 64),), jnp.float32)
    column_factor_stack = normal_values(keys[3], (LEVELS, POINTS, RANK), POINTS ** -0.5, 0.0234375, ((1, 64),), jnp.float32)
    probes = normal_values(keys[4], (POINTS, PROBES), 1.0, 6.0, ((0, 64), (1, 4)), jnp.float32)
    return {"leaf_blocks": leaf_blocks, "block_mask": block_mask, "row_factor_stack": row_factor_stack, "column_factor_stack": column_factor_stack, "probes": probes}


def leaf_product(inputs):
    block, weights, columns = inputs
    block_span_width = LEAF_PTS // MB
    spread = jnp.repeat(jnp.repeat(weights.astype(jnp.float32), block_span_width, 0), block_span_width, 1)
    return jnp.dot(block * spread, columns, precision=lax.Precision.HIGHEST, preferred_element_type=jnp.float32)


def reference(leaf_blocks, block_mask, row_factor_stack, column_factor_stack, probes):
    block_list = leaf_blocks.reshape(N_LEAF, LEAF_PTS, LEAF_PTS)
    columns = probes.reshape(N_LEAF, LEAF_PTS, PROBES)
    applied = lax.map(leaf_product, (block_list, block_mask, columns)).reshape(POINTS, PROBES)
    for level in range(LEVELS):
        width = LEAF_PTS * 2 ** level
        cluster_groups = POINTS // width
        grouped = probes.reshape(cluster_groups, width, PROBES)
        right_part = column_factor_stack[level].reshape(cluster_groups, width, RANK)
        probe_projected = jnp.einsum("bsr,bsp->brp", right_part, grouped, precision=lax.Precision.HIGHEST)
        swapped = probe_projected.reshape(cluster_groups // 2, 2, RANK, PROBES)[:, ::-1].reshape(cluster_groups, RANK, PROBES)
        left_part = row_factor_stack[level].reshape(cluster_groups, width, RANK)
        applied = applied + jnp.einsum("bsr,brp->bsp", left_part, swapped, precision=lax.Precision.HIGHEST).reshape(POINTS, PROBES)
    probe_gram = jnp.dot(applied.T, applied, precision=lax.Precision.HIGHEST, preferred_element_type=jnp.float32) / POINTS
    return applied, probe_gram
```

```python
import jax
import jax.numpy as jnp
from jax import lax
from jax.sharding import PartitionSpec as P

HIGH = lax.Precision.HIGH


def swap(value, axis, mask):
    pairs = [(source, source ^ mask) for source in range(lax.axis_size(axis))]
    return lax.ppermute(value, axis, pairs)


def halves(value, axis, bit):
    size = value.shape[axis] // 2
    keep = lax.dynamic_slice_in_dim(value, bit * size, size, axis)
    give = lax.dynamic_slice_in_dim(value, (1 - bit) * size, size, axis)
    return keep, give


def join(own, other, axis, bit):
    first = jnp.where(bit == 0, own, other)
    second = jnp.where(bit == 0, other, own)
    return jnp.concatenate([first, second], axis)


def project(columns, probes):
    return jnp.einsum("tec,eg->tcg", columns, probes, precision=HIGH)


def expand(rows, nodes):
    return jnp.einsum("tvi,tic->vc", rows, nodes, precision=HIGH)


def local(leaf_blocks, block_mask, row_factor_stack, column_factor_stack, probes):
    leaf_points = leaf_blocks.shape[1]
    side = block_mask.shape[1]
    span = leaf_points // side
    leaf = lax.axis_index("leaf")
    probe = lax.axis_index("probe")
    bit = [(leaf >> k) & 1 for k in range(6)]

    high = project(column_factor_stack[3:6], probes)
    keep, give = halves(high, 1, bit[2])
    high = keep + swap(give, "leaf", 4)
    keep, give = halves(high[1:], 1, bit[3])
    sent = jnp.concatenate([high[0], give.reshape(64, -1)])
    got = swap(sent, "leaf", 8)
    three = got[:64]
    upper = keep.reshape(64, -1) + got[64:]
    got = swap(upper, "leaf", 16)
    four = got[:32]
    five = upper[32:] + got[32:]
    five = swap(five, "leaf", 32)
    part = jnp.concatenate([three, four, five])
    low = project(column_factor_stack[:3], probes)
    got = swap(jnp.stack([low[0], low[2]]), "leaf", 1)
    zero = got[0]
    two = low[2] + got[1]
    two = two + swap(two, "leaf", 2)
    two = swap(two, "leaf", 4)
    part = part + swap(part, "leaf", 1)
    part = part + swap(part, "leaf", 2)
    upper = part[64:].reshape(2, 32, -1)
    upper = join(upper, swap(upper, "leaf", 8), 1, bit[3])
    high = jnp.concatenate([part[None, :64], upper])
    high = join(high, swap(high, "leaf", 4), 1, bit[2])
    one = low[1] + swap(low[1], "leaf", 1)
    one = swap(one, "leaf", 2)

    weights = block_mask[0].astype(jnp.float32)
    masked = (
        leaf_blocks.reshape(side, span, side, span) * weights[:, None, :, None]
    ).reshape(leaf_points, leaf_points)
    near = jnp.dot(masked, probes, precision=HIGH, preferred_element_type=jnp.float32)
    nodes = jnp.concatenate([jnp.stack([zero, one, two]), high])
    applied = near + expand(row_factor_stack, nodes)

    def gram(other):
        return lax.dot_general(
            other, applied, (((0,), (0,)), ((), ())), precision=HIGH,
            preferred_element_type=jnp.float32,
        )

    def scatter_x(block):
        keep, give = halves(block, 0, bit[3])
        block = keep + swap(give, "leaf", 8)
        keep, give = halves(block, 0, bit[2])
        return keep + swap(give, "leaf", 4)

    beside = swap(applied, "probe", 1)
    width = applied.shape[1] // 2
    far = [swap(applied[:, h * width:(h + 1) * width], "probe", 2) for h in range(2)]
    blocks = scatter_x(gram(applied)), scatter_x(gram(beside))
    across = [swap(half, "probe", 1) for half in far]
    far = jnp.concatenate(far, 1)
    across = jnp.concatenate(across, 1)
    blocks += scatter_x(gram(far)), scatter_x(gram(across))
    total = jnp.stack(blocks).reshape(2, 2, 64, -1)
    keep, give = halves(total, 0, bit[5] ^ (probe >> 1))
    total = (keep + swap(give, "leaf", 32))[0]
    keep, give = halves(total, 0, bit[4] ^ (probe & 1))
    total = (keep + swap(give, "leaf", 16))[0]
    keep, give = halves(total, 0, bit[1])
    total = keep + swap(give, "leaf", 2)
    keep, give = halves(total, 0, bit[0])
    total = keep + swap(give, "leaf", 1)
    total_points = leaf_points * lax.axis_size("leaf")
    return applied, total / total_points


def solution(mesh):
    return jax.shard_map(
        local,
        mesh=mesh,
        in_specs=(
            P("leaf", None),
            P("leaf", None, None),
            P(None, "leaf", None),
            P(None, "leaf", None),
            P("leaf", "probe"),
        ),
        out_specs=(P("leaf", "probe"), P("leaf", "probe")),
        check_vma=False,
    )
```

```python
import functools

import jax
import jax.numpy as jnp
from jax import lax
from jax.experimental import pallas as pl
from jax.experimental.pallas import tpu as pltpu
from jax.sharding import PartitionSpec as P

HIGH = lax.Precision.HIGH
F32 = jnp.float32
LIMIT = 40 * 2**20


def swap(value, axis, mask):
    pairs = [(source, source ^ mask) for source in range(lax.axis_size(axis))]
    return lax.ppermute(value, axis, pairs)


def split(value):
    top = value.astype(jnp.bfloat16)
    return top, (value - top.astype(F32)).astype(jnp.bfloat16)


def dot3(left, right, dims):
    dot = functools.partial(
        lax.dot_general, dimension_numbers=(dims, ((), ())), preferred_element_type=F32
    )
    return dot(left[0], right[0]) + (dot(left[0], right[1]) + dot(left[1], right[0]))


ROWS = ((0,), (0,))
MATMUL = ((1,), (0,))


def whole(shape):
    return pl.BlockSpec(shape, lambda *_: (0,) * len(shape))


def shapes(*dims):
    return [jax.ShapeDtypeStruct(d, F32) for d in dims]


def call(body, outs, specs, operands, scratch=(), flops=0, grid=(1,), out_specs=None):
    moved = sum(o.size * 4 for o in operands) + sum(o.size * 4 for o in outs)
    return pl.pallas_call(
        body,
        out_shape=outs,
        grid=grid,
        in_specs=specs,
        out_specs=[whole(o.shape) for o in outs] if out_specs is None else out_specs,
        scratch_shapes=list(scratch),
        compiler_params=pltpu.CompilerParams(vmem_limit_bytes=LIMIT),
        cost_estimate=pl.CostEstimate(flops=flops, bytes_accessed=moved, transcendentals=0),
    )(*operands)


def place():
    leaf = lax.axis_index("leaf")
    return leaf >> 4, (leaf >> 2) & 3, leaf & 3


def project_high(columns, probes):
    def body(c_ref, p_ref, keep, one, two, three, total):
        _, x, _ = place()
        right = split(p_ref[...])
        for level in range(3):
            total[level] = dot3(split(c_ref[level]), right, ROWS)
        for part, out in ((1, one), (2, two), (3, three)):
            base = 0 if part == 1 else 64
            if part > 1:
                half = ((x ^ part) & 1) * 64
                out[:64] = total[0, pl.ds(pl.multiple_of(half, 64), 64)]
            row = pl.multiple_of((x ^ part) * 32, 32)
            out[base:base + 32] = total[1, pl.ds(row, 32)]
            out[base + 32:base + 64] = total[2, pl.ds(row, 32)]
        row = pl.multiple_of(x * 32, 32)
        keep[:32] = total[1, pl.ds(row, 32)]
        keep[32:] = total[2, pl.ds(row, 32)]

    _, points, rank = columns.shape
    wide = probes.shape[1]
    return call(
        body,
        shapes((64, wide), (64, wide), (128, wide), (128, wide)),
        [pl.BlockSpec((3, points, rank), lambda _: (1, 0, 0)), whole(probes.shape)],
        [columns, probes],
        [pltpu.VMEM((3, rank, wide), F32)],
        flops=18 * points * rank * wide,
    )


def project_low(columns, probes):
    def body(c_ref, p_ref, pair, one):
        right = split(p_ref[...])
        pair[0] = dot3(split(c_ref[0]), right, ROWS)
        pair[1] = dot3(split(c_ref[2]), right, ROWS)
        one[...] = dot3(split(c_ref[1]), right, ROWS)

    _, points, rank = columns.shape
    wide = probes.shape[1]
    return call(
        body,
        shapes((2, rank, wide), (rank, wide)),
        [pl.BlockSpec((3, points, rank), lambda _: (0, 0, 0)), whole(probes.shape)],
        [columns, probes],
        flops=18 * points * rank * wide,
    )


def expand(near, rows, zero, one, two, part, part1, part2, part3):
    def body(n_ref, u_ref, z_ref, o_ref, t_ref, q0, q1, q2, q3, out, total, high, low):
        _, x, _ = place()

        @pl.when(pl.program_id(0) == 0)
        def _():
            total[0:128] = z_ref[...]
            total[128:256] = o_ref[...]
            total[256:384] = t_ref[...]
            for k, ref in ((0, q0), (1, q1)):
                total[pl.ds(pl.multiple_of(384 + ((x ^ k) & 1) * 64, 64), 64)] = ref[:64]
            for k, ref in ((0, q0), (1, q1), (2, q2), (3, q3)):
                base = 64 if k < 2 else 0
                row = pl.multiple_of((x ^ k) * 32, 32)
                total[pl.ds(512 + row, 32)] = ref[base:base + 32]
                total[pl.ds(640 + row, 32)] = ref[base + 32:base + 64]
            high[...], low[...] = split(total[...])

        left = jnp.concatenate([u_ref[t] for t in range(6)], axis=1)
        out[...] = n_ref[...] + dot3(split(left), (high[...], low[...]), MATMUL)

    levels, points, rank = rows.shape
    wide = near.shape[1]
    tile = 256
    nodes = [zero, one, two, part, part1, part2, part3]
    return call(
        body,
        shapes(near.shape),
        [
            pl.BlockSpec((tile, wide), lambda i: (i, 0)),
            pl.BlockSpec((levels, tile, rank), lambda i: (0, i, 0)),
        ] + [whole(n.shape) for n in nodes],
        [near, rows] + nodes,
        [
            pltpu.VMEM((levels * rank, wide), F32),
            pltpu.VMEM((levels * rank, wide), jnp.bfloat16),
            pltpu.VMEM((levels * rank, wide), jnp.bfloat16),
        ],
        flops=6 * levels * rank * points * wide,
        grid=(points // tile,),
        out_specs=[pl.BlockSpec((tile, wide), lambda i: (i, 0))],
    )[0]


def gram(others, applied):
    wide = applied.shape[1]
    given = [applied] if others[0] is applied else [applied, others[0]]
    given = given + [others[1]]

    def body(*refs):
        (a_ref, first), second = (refs[0], refs[len(given) - 2]), refs[len(given) - 1]
        outs, total = refs[len(given):-1], refs[-1]
        _, x, _ = place()
        right = split(a_ref[...])
        left = right if first is a_ref else split(first[...])
        total[0] = dot3(left, right, ROWS)
        total[1] = dot3(split(second[...]), right, ROWS)
        for k, out in enumerate(outs):
            row = pl.multiple_of((x ^ k) * (wide // 4), wide // 4)
            out[...] = total[:, pl.ds(row, wide // 4)]

    return call(
        body,
        shapes(*[(2, wide // 4, wide)] * 4),
        [whole(g.shape) for g in given],
        given,
        [pltpu.VMEM((2, wide, wide), F32)],
        flops=12 * wide * wide * applied.shape[0],
    )


def cut_y(near, far):
    _, rows, wide = near[0].shape

    def body(*refs):
        ins, outs, total = refs[:8], refs[8:12], refs[12]
        y, _, _ = place()
        probe = lax.axis_index("probe")
        total[:2] = (ins[0][...] + ins[1][...]) + (ins[2][...] + ins[3][...])
        total[2:] = (ins[4][...] + ins[5][...]) + (ins[6][...] + ins[7][...])
        for k, out in enumerate(outs):
            out[...] = total[probe ^ y ^ k]

    ins = [*near, *far]
    return call(
        body,
        shapes(*[(rows, wide)] * 4),
        [whole(i.shape) for i in ins],
        ins,
        [pltpu.VMEM((4, rows, wide), F32)],
    )


def cut_z(ins):
    rows, wide = ins[0].shape

    def body(*refs):
        ins, outs, total = refs[:4], refs[4:8], refs[8]
        _, _, z = place()
        total[...] = (ins[0][...] + ins[1][...]) + (ins[2][...] + ins[3][...])
        for k, out in enumerate(outs):
            out[...] = total[pl.ds(pl.multiple_of((z ^ k) * (rows // 4), rows // 4), rows // 4)]

    return call(
        body,
        shapes(*[(rows // 4, wide)] * 4),
        [whole(i.shape) for i in ins],
        list(ins),
        [pltpu.VMEM((rows, wide), F32)],
    )


def around(parts, scale):
    return [parts[0]] + [swap(parts[k], "leaf", k * scale) for k in (1, 2, 3)]


def local(leaf_blocks, block_mask, row_factor_stack, column_factor_stack, probes):
    leaf_points = leaf_blocks.shape[1]
    side = block_mask.shape[1]
    span = leaf_points // side

    keep, *sent = project_high(column_factor_stack, probes)
    _, one, two, three = around([keep, *sent], 4)
    pair, low1 = project_low(column_factor_stack, probes)
    got = swap(pair, "leaf", 1)
    node0, node2 = got[0], pair[1] + got[1]
    part3 = two[:64] + three[:64]
    upper = keep + one + two[64:] + three[64:]
    part4 = swap(upper[:32], "leaf", 16)
    five = upper[32:]
    part5 = swap(five, "leaf", 32) + swap(five, "leaf", 48)
    part = jnp.concatenate([part3, part4, part5])
    node2 = node2 + swap(node2, "leaf", 2)
    node2 = swap(node2, "leaf", 4)
    part = part + swap(part, "leaf", 1)
    part = part + swap(part, "leaf", 2)
    gathered = [swap(part, "leaf", 4), swap(part[64:], "leaf", 8), swap(part[64:], "leaf", 12)]
    node1 = low1 + swap(low1, "leaf", 1)
    node1 = swap(node1, "leaf", 2)

    weights = block_mask[0].astype(F32)
    masked = (
        leaf_blocks.reshape(side, span, side, span) * weights[:, None, :, None]
    ).reshape(leaf_points, leaf_points)
    near = jnp.dot(masked, probes, precision=HIGH, preferred_element_type=F32)
    applied = expand(near, row_factor_stack, node0, node1, node2, part, *gathered)

    far = swap(applied, "probe", 2)
    beside = swap(applied, "probe", 1)
    first = around(gram([applied, beside], applied), 4)
    far, *first = lax.optimization_barrier((far, *first))
    across = swap(far, "probe", 1)
    second = around(gram([far, across], applied), 4)
    blocks = around(cut_y(first, second), 16)
    blocks = around(cut_z(blocks), 1)
    total = (blocks[0] + blocks[1]) + (blocks[2] + blocks[3])
    return applied, total / (leaf_points * lax.axis_size("leaf"))


def solution(mesh):
    return jax.shard_map(
        local,
        mesh=mesh,
        in_specs=(
            P("leaf", None),
            P("leaf", None, None),
            P(None, "leaf", None),
            P(None, "leaf", None),
            P("leaf", "probe"),
        ),
        out_specs=(P("leaf", "probe"), P("leaf", "probe")),
        check_vma=False,
    )
```

```python
import functools

import jax
import jax.numpy as jnp
from jax import lax
from jax.experimental import pallas as pl
from jax.experimental.pallas import tpu as pltpu
from jax.sharding import PartitionSpec as P

HIGH = lax.Precision.HIGH
F32 = jnp.float32
LIMIT = 40 * 2**20
MOST = 52 * 2**20


def swap(value, axis, mask):
    pairs = [(source, source ^ mask) for source in range(lax.axis_size(axis))]
    return lax.ppermute(value, axis, pairs)


def split(value):
    top = value.astype(jnp.bfloat16)
    return top, (value - top.astype(F32)).astype(jnp.bfloat16)


def dot3(left, right, dims):
    dot = functools.partial(
        lax.dot_general, dimension_numbers=(dims, ((), ())), preferred_element_type=F32
    )
    return dot(left[0], right[0]) + (dot(left[0], right[1]) + dot(left[1], right[0]))


ROWS = ((0,), (0,))
MATMUL = ((1,), (0,))


def whole(shape):
    return pl.BlockSpec(shape, lambda *_: (0,) * len(shape))


def shapes(*dims):
    return [jax.ShapeDtypeStruct(d, F32) for d in dims]


def call(
    body, outs, specs, operands, scratch=(), flops=0, grid=(1,), out_specs=None, limit=LIMIT
):
    moved = sum(o.size * 4 for o in operands) + sum(o.size * 4 for o in outs)
    return pl.pallas_call(
        body,
        out_shape=outs,
        grid=grid,
        in_specs=specs,
        out_specs=[whole(o.shape) for o in outs] if out_specs is None else out_specs,
        scratch_shapes=list(scratch),
        compiler_params=pltpu.CompilerParams(vmem_limit_bytes=limit),
        cost_estimate=pl.CostEstimate(flops=flops, bytes_accessed=moved, transcendentals=0),
    )(*operands)


def place():
    leaf = lax.axis_index("leaf")
    return leaf >> 4, (leaf >> 2) & 3, leaf & 3


def project_high(columns, probes):
    def body(c_ref, p_ref, keep, one, two, three, total):
        _, x, _ = place()
        right = split(p_ref[...])
        for level in range(3):
            total[level] = dot3(split(c_ref[level]), right, ROWS)
        for part, out in ((1, one), (2, two), (3, three)):
            base = 0 if part == 1 else 64
            if part > 1:
                half = ((x ^ part) & 1) * 64
                out[:64] = total[0, pl.ds(pl.multiple_of(half, 64), 64)]
            row = pl.multiple_of((x ^ part) * 32, 32)
            out[base:base + 32] = total[1, pl.ds(row, 32)]
            out[base + 32:base + 64] = total[2, pl.ds(row, 32)]
        row = pl.multiple_of(x * 32, 32)
        keep[:32] = total[1, pl.ds(row, 32)]
        keep[32:] = total[2, pl.ds(row, 32)]

    _, points, rank = columns.shape
    wide = probes.shape[1]
    return call(
        body,
        shapes((64, wide), (64, wide), (128, wide), (128, wide)),
        [pl.BlockSpec((3, points, rank), lambda _: (1, 0, 0)), whole(probes.shape)],
        [columns, probes],
        [pltpu.VMEM((3, rank, wide), F32)],
        flops=18 * points * rank * wide,
        limit=MOST,
    )


def project_low(columns, probes):
    def body(c_ref, p_ref, *outs):
        right = split(p_ref[...])
        for level, out in enumerate(outs):
            out[...] = dot3(split(c_ref[level]), right, ROWS)

    _, points, rank = columns.shape
    wide = probes.shape[1]
    return call(
        body,
        shapes(*[(rank, wide)] * 3),
        [pl.BlockSpec((3, points, rank), lambda _: (0, 0, 0)), whole(probes.shape)],
        [columns, probes],
        flops=18 * points * rank * wide,
        limit=LIMIT,
    )


LATE = (1, 3, 4, 5)


def prepare(near, rows, zero, two):
    def body(n_ref, u_ref, z_ref, t_ref, out, high, low):
        early = jnp.concatenate([u_ref[0], u_ref[2]], axis=1)
        nodes = jnp.concatenate([z_ref[...], t_ref[...]], axis=0)
        out[...] = n_ref[...] + dot3(split(early), split(nodes), MATMUL)
        high[...], low[...] = split(jnp.concatenate([u_ref[t] for t in LATE], axis=1))

    levels, points, rank = rows.shape
    wide = near.shape[1]
    tile = 256

    def tiled(width):
        return pl.BlockSpec((tile, width), lambda i: (i, 0))

    late = jax.ShapeDtypeStruct((points, len(LATE) * rank), jnp.bfloat16)
    return call(
        body,
        shapes(near.shape) + [late, late],
        [
            tiled(wide),
            pl.BlockSpec((levels, tile, rank), lambda i: (0, i, 0)),
            whole(zero.shape),
            whole(two.shape),
        ],
        [near, rows, zero, two],
        flops=12 * rank * points * wide,
        grid=(points // tile,),
        out_specs=[tiled(wide), tiled(len(LATE) * rank), tiled(len(LATE) * rank)],
    )


def expand(base, rows_high, rows_low, one, part, part1, part2, part3):
    def body(b_ref, h_ref, l_ref, o_ref, q0, q1, q2, q3, out, held, total):
        _, x, _ = place()
        total[0:128] = o_ref[...]
        for k, ref in ((0, q0), (1, q1)):
            total[pl.ds(pl.multiple_of(128 + ((x ^ k) & 1) * 64, 64), 64)] = ref[:64]
        for k, ref in ((0, q0), (1, q1), (2, q2), (3, q3)):
            base = 64 if k < 2 else 0
            row = pl.multiple_of((x ^ k) * 32, 32)
            total[pl.ds(256 + row, 32)] = ref[base:base + 32]
            total[pl.ds(384 + row, 32)] = ref[base + 32:base + 64]
        left = h_ref[...], l_ref[...]
        held[...] = b_ref[...] + dot3(left, split(total[...]), MATMUL)
        out[...] = held[...]

    points, wide = base.shape
    depth = rows_high.shape[1]
    given = [base, rows_high, rows_low, one, part, part1, part2, part3]
    return call(
        body,
        shapes(base.shape, base.shape),
        [whole(g.shape) for g in given],
        given,
        [pltpu.VMEM((depth, wide), F32)],
        flops=6 * depth * points * wide,
    )


def gram(others, applied):
    wide = applied.shape[1]
    given = [applied] if others[0] is applied else [applied, others[0]]
    given = given + [others[1]]

    def body(*refs):
        (a_ref, first), second = (refs[0], refs[len(given) - 2]), refs[len(given) - 1]
        outs, total = refs[len(given):-1], refs[-1]
        _, x, _ = place()
        right = split(a_ref[...])
        left = right if first is a_ref else split(first[...])
        total[0] = dot3(left, right, ROWS)
        total[1] = dot3(split(second[...]), right, ROWS)
        for k, out in enumerate(outs):
            row = pl.multiple_of((x ^ k) * (wide // 4), wide // 4)
            out[...] = total[:, pl.ds(row, wide // 4)]

    return call(
        body,
        shapes(*[(2, wide // 4, wide)] * 4),
        [whole(g.shape) for g in given],
        given,
        [pltpu.VMEM((2, wide, wide), F32)],
        flops=12 * wide * wide * applied.shape[0],
    )


def cut_y(near, far):
    _, rows, wide = near[0].shape

    def body(*refs):
        ins, outs, total = refs[:8], refs[8:12], refs[12]
        y, _, _ = place()
        probe = lax.axis_index("probe")
        total[:2] = (ins[0][...] + ins[1][...]) + (ins[2][...] + ins[3][...])
        total[2:] = (ins[4][...] + ins[5][...]) + (ins[6][...] + ins[7][...])
        for k, out in enumerate(outs):
            out[...] = total[probe ^ y ^ k]

    ins = [*near, *far]
    return call(
        body,
        shapes(*[(rows, wide)] * 4),
        [whole(i.shape) for i in ins],
        ins,
        [pltpu.VMEM((4, rows, wide), F32)],
    )


def cut_z(ins):
    rows, wide = ins[0].shape

    def body(*refs):
        ins, outs, total = refs[:4], refs[4:8], refs[8]
        _, _, z = place()
        total[...] = (ins[0][...] + ins[1][...]) + (ins[2][...] + ins[3][...])
        for k, out in enumerate(outs):
            out[...] = total[pl.ds(pl.multiple_of((z ^ k) * (rows // 4), rows // 4), rows // 4)]

    return call(
        body,
        shapes(*[(rows // 4, wide)] * 4),
        [whole(i.shape) for i in ins],
        list(ins),
        [pltpu.VMEM((rows, wide), F32)],
    )


def around(parts, scale):
    return [parts[0]] + [swap(parts[k], "leaf", k * scale) for k in (1, 2, 3)]


def local(leaf_blocks, block_mask, row_factor_stack, column_factor_stack, probes):
    leaf_points = leaf_blocks.shape[1]
    side = block_mask.shape[1]
    span = leaf_points // side

    weights = block_mask[0].astype(F32)
    masked = (
        leaf_blocks.reshape(side, span, side, span) * weights[:, None, :, None]
    ).reshape(leaf_points, leaf_points)
    near = jnp.dot(masked, probes, precision=HIGH, preferred_element_type=F32)

    keep, *sent = project_high(column_factor_stack, probes)
    _, one, two, three = around([keep, *sent], 4)
    low0, low1, low2 = project_low(column_factor_stack, probes)
    two_a = swap(low2, "leaf", 3)
    one_a = swap(low1, "leaf", 2)
    node0 = swap(low0, "leaf", 1)
    low2 = low2 + two_a
    part3 = two[:64] + three[:64]
    upper = keep + one + two[64:] + three[64:]
    part4 = swap(upper[:32], "leaf", 16)
    five = upper[32:]
    part5 = swap(five, "leaf", 32) + swap(five, "leaf", 48)
    part = jnp.concatenate([part3, part4, part5])
    node2 = low2 + swap(low2, "leaf", 2)
    node2 = swap(node2, "leaf", 4)
    part, node0, one_a = lax.optimization_barrier((part, node0, one_a))
    part = part + swap(part, "leaf", 1)
    part, near = lax.optimization_barrier((part, near))
    part = part + swap(part, "leaf", 2)
    late = prepare(near, row_factor_stack, node0, node2)
    part, low1, *late = lax.optimization_barrier((part, low1, *late))
    gathered = [swap(part, "leaf", 4), swap(part[64:], "leaf", 8), swap(part[64:], "leaf", 12)]
    node1 = one_a + swap(low1, "leaf", 3)

    result, applied = expand(*late, node1, part, *gathered)

    far = swap(applied, "probe", 2)
    beside = swap(applied, "probe", 1)
    first = around(gram([applied, beside], applied), 4)
    far, *first = lax.optimization_barrier((far, *first))
    across = swap(far, "probe", 1)
    second = around(gram([far, across], applied), 4)
    blocks = around(cut_y(first, second), 16)
    blocks = around(cut_z(blocks), 1)
    total = (blocks[0] + blocks[1]) + (blocks[2] + blocks[3])
    return result, total / (leaf_points * lax.axis_size("leaf"))


def solution(mesh):
    return jax.shard_map(
        local,
        mesh=mesh,
        in_specs=(
            P("leaf", None),
            P("leaf", None, None),
            P(None, "leaf", None),
            P(None, "leaf", None),
            P("leaf", "probe"),
        ),
        out_specs=(P("leaf", "probe"), P("leaf", "probe")),
        check_vma=False,
    )
```

```python
import functools

import jax
import jax.numpy as jnp
from jax import lax
from jax.experimental import pallas as pl
from jax.experimental.pallas import tpu as pltpu
from jax.sharding import PartitionSpec as P

HIGH = lax.Precision.HIGH
F32 = jnp.float32
LIMIT = 40 * 2**20
MOST = 53 * 2**20


def swap(value, axis, mask):
    pairs = [(source, source ^ mask) for source in range(lax.axis_size(axis))]
    return lax.ppermute(value, axis, pairs)


def split(value):
    top = value.astype(jnp.bfloat16)
    return top, (value - top.astype(F32)).astype(jnp.bfloat16)


def dot3(left, right, dims):
    dot = functools.partial(
        lax.dot_general, dimension_numbers=(dims, ((), ())), preferred_element_type=F32
    )
    return dot(left[0], right[0]) + (dot(left[0], right[1]) + dot(left[1], right[0]))


ROWS = ((0,), (0,))
MATMUL = ((1,), (0,))


def whole(shape):
    return pl.BlockSpec(shape, lambda *_: (0,) * len(shape))


def shapes(*dims):
    return [jax.ShapeDtypeStruct(d, F32) for d in dims]


def call(
    body, outs, specs, operands, scratch=(), flops=0, grid=(1,), out_specs=None, limit=LIMIT
):
    moved = sum(o.size * 4 for o in operands) + sum(o.size * 4 for o in outs)
    return pl.pallas_call(
        body,
        out_shape=outs,
        grid=grid,
        in_specs=specs,
        out_specs=[whole(o.shape) for o in outs] if out_specs is None else out_specs,
        scratch_shapes=list(scratch),
        compiler_params=pltpu.CompilerParams(vmem_limit_bytes=limit),
        cost_estimate=pl.CostEstimate(flops=flops, bytes_accessed=moved, transcendentals=0),
    )(*operands)


def place():
    leaf = lax.axis_index("leaf")
    return leaf >> 4, (leaf >> 2) & 3, leaf & 3


def project(columns, probes, levels, outs, emit):
    _, points, rank = columns.shape
    wide = probes.shape[1]
    first = levels[0]

    def body(c_hbm, p_hbm, *refs):
        *results, held, given, sems = refs
        copies = [pltpu.make_async_copy(p_hbm, given, sems.at[0])]
        for k, level in enumerate(levels):
            copies.append(pltpu.make_async_copy(c_hbm.at[level], held.at[k], sems.at[k + 1]))
        for copy in copies:
            copy.start()
        copies[0].wait()
        right = split(given[...])
        for k, level in enumerate(levels):
            copies[k + 1].wait()
            emit(level - first, dot3(split(held[k]), right, ROWS), *results)

    return call(
        body,
        outs,
        [pl.BlockSpec(memory_space=pltpu.HBM)] * 2,
        [columns, probes],
        [
            pltpu.VMEM((len(levels), points, rank), F32),
            pltpu.VMEM((points, wide), F32),
            pltpu.SemaphoreType.DMA((len(levels) + 1,)),
        ],
        flops=6 * len(levels) * points * rank * wide,
        limit=MOST,
    )


def project_high(columns, probes):
    def emit(level, value, keep, one, two, three, total):
        _, x, _ = place()
        total[...] = value
        if level == 0:
            for part, out in ((2, two), (3, three)):
                half = ((x ^ part) & 1) * 64
                out[:64] = total[pl.ds(pl.multiple_of(half, 64), 64)]
            return
        low = (level - 1) * 32
        for part, base, out in ((0, 0, keep), (1, 0, one), (2, 64, two), (3, 64, three)):
            row = pl.multiple_of((x ^ part) * 32, 32)
            out[base + low:base + low + 32] = total[pl.ds(row, 32)]

    rank, wide = columns.shape[2], probes.shape[1]
    outs = shapes((64, wide), (64, wide), (128, wide), (128, wide), (rank, wide))
    return project(columns, probes, (3, 4, 5), outs, emit)[:4]


def project_low(columns, probes):
    def emit(level, value, *outs):
        outs[level][...] = value

    outs = shapes(*[(columns.shape[2], probes.shape[1])] * 3)
    return project(columns, probes, (0, 1, 2), outs, emit)


LATE = (1, 3, 4, 5)


def prepare(near, rows, zero, two):
    def body(n_ref, u_ref, z_ref, t_ref, out, high, low):
        early = jnp.concatenate([u_ref[0], u_ref[2]], axis=1)
        nodes = jnp.concatenate([z_ref[...], t_ref[...]], axis=0)
        out[...] = n_ref[...] + dot3(split(early), split(nodes), MATMUL)
        high[...], low[...] = split(jnp.concatenate([u_ref[t] for t in LATE], axis=1))

    levels, points, rank = rows.shape
    wide = near.shape[1]
    tile = 256

    def tiled(width):
        return pl.BlockSpec((tile, width), lambda i: (i, 0))

    late = jax.ShapeDtypeStruct((points, len(LATE) * rank), jnp.bfloat16)
    return call(
        body,
        shapes(near.shape) + [late, late],
        [
            tiled(wide),
            pl.BlockSpec((levels, tile, rank), lambda i: (0, i, 0)),
            whole(zero.shape),
            whole(two.shape),
        ],
        [near, rows, zero, two],
        flops=12 * rank * points * wide,
        grid=(points // tile,),
        out_specs=[tiled(wide), tiled(len(LATE) * rank), tiled(len(LATE) * rank)],
    )


def expand(base, rows_high, rows_low, one, part, part1, part2, part3):
    def body(b_ref, h_ref, l_ref, o_ref, q0, q1, q2, q3, out, held, total):
        _, x, _ = place()
        total[0:128] = o_ref[...]
        for k, ref in ((0, q0), (1, q1)):
            total[pl.ds(pl.multiple_of(128 + ((x ^ k) & 1) * 64, 64), 64)] = ref[:64]
        for k, ref in ((0, q0), (1, q1), (2, q2), (3, q3)):
            base = 64 if k < 2 else 0
            row = pl.multiple_of((x ^ k) * 32, 32)
            total[pl.ds(256 + row, 32)] = ref[base:base + 32]
            total[pl.ds(384 + row, 32)] = ref[base + 32:base + 64]
        left = h_ref[...], l_ref[...]
        held[...] = b_ref[...] + dot3(left, split(total[...]), MATMUL)
        out[...] = held[...]

    points, wide = base.shape
    depth = rows_high.shape[1]
    given = [base, rows_high, rows_low, one, part, part1, part2, part3]
    return call(
        body,
        shapes(base.shape, base.shape),
        [whole(g.shape) for g in given],
        given,
        [pltpu.VMEM((depth, wide), F32)],
        flops=6 * depth * points * wide,
    )


def gram(others, applied):
    wide = applied.shape[1]
    given = [applied] if others[0] is applied else [applied, others[0]]
    given = given + [others[1]]

    def body(*refs):
        (a_ref, first), second = (refs[0], refs[len(given) - 2]), refs[len(given) - 1]
        outs, total = refs[len(given):-1], refs[-1]
        _, x, _ = place()
        right = split(a_ref[...])
        left = right if first is a_ref else split(first[...])
        total[0] = dot3(left, right, ROWS)
        total[1] = dot3(split(second[...]), right, ROWS)
        for k, out in enumerate(outs):
            row = pl.multiple_of((x ^ k) * (wide // 4), wide // 4)
            out[...] = total[:, pl.ds(row, wide // 4)]

    return call(
        body,
        shapes(*[(2, wide // 4, wide)] * 4),
        [whole(g.shape) for g in given],
        given,
        [pltpu.VMEM((2, wide, wide), F32)],
        flops=12 * wide * wide * applied.shape[0],
    )


def cut_y(near, far):
    _, rows, wide = near[0].shape

    def body(*refs):
        ins, outs, total = refs[:8], refs[8:12], refs[12]
        y, _, _ = place()
        probe = lax.axis_index("probe")
        total[:2] = (ins[0][...] + ins[1][...]) + (ins[2][...] + ins[3][...])
        total[2:] = (ins[4][...] + ins[5][...]) + (ins[6][...] + ins[7][...])
        for k, out in enumerate(outs):
            out[...] = total[probe ^ y ^ k]

    ins = [*near, *far]
    return call(
        body,
        shapes(*[(rows, wide)] * 4),
        [whole(i.shape) for i in ins],
        ins,
        [pltpu.VMEM((4, rows, wide), F32)],
    )


def cut_z(ins):
    rows, wide = ins[0].shape

    def body(*refs):
        ins, outs, total = refs[:4], refs[4:8], refs[8]
        _, _, z = place()
        total[...] = (ins[0][...] + ins[1][...]) + (ins[2][...] + ins[3][...])
        for k, out in enumerate(outs):
            out[...] = total[pl.ds(pl.multiple_of((z ^ k) * (rows // 4), rows // 4), rows // 4)]

    return call(
        body,
        shapes(*[(rows // 4, wide)] * 4),
        [whole(i.shape) for i in ins],
        list(ins),
        [pltpu.VMEM((rows, wide), F32)],
    )


def around(parts, scale):
    return [parts[0]] + [swap(parts[k], "leaf", k * scale) for k in (1, 2, 3)]


def local(leaf_blocks, block_mask, row_factor_stack, column_factor_stack, probes):
    leaf_points = leaf_blocks.shape[1]
    side = block_mask.shape[1]
    span = leaf_points // side

    weights = block_mask[0].astype(F32)
    masked = (
        leaf_blocks.reshape(side, span, side, span) * weights[:, None, :, None]
    ).reshape(leaf_points, leaf_points)
    near = jnp.dot(masked, probes, precision=HIGH, preferred_element_type=F32)

    keep, *sent = project_high(column_factor_stack, probes)
    _, one, two, three = around([keep, *sent], 4)
    low0, low1, low2 = project_low(column_factor_stack, probes)
    two_a = swap(low2, "leaf", 3)
    node0 = swap(low0, "leaf", 1)
    low2 = low2 + two_a
    part3 = two[:64] + three[:64]
    upper = keep + one + two[64:] + three[64:]
    part4 = swap(upper[:32], "leaf", 16)
    five = upper[32:]
    part5 = swap(five, "leaf", 32) + swap(five, "leaf", 48)
    part = jnp.concatenate([part3, part4, part5])
    node2 = low2 + swap(low2, "leaf", 2)
    node2 = swap(node2, "leaf", 4)
    part, node0 = lax.optimization_barrier((part, node0))
    part = part + swap(part, "leaf", 1)
    part, near = lax.optimization_barrier((part, near))
    part = part + swap(part, "leaf", 2)
    late = prepare(near, row_factor_stack, node0, node2)
    part, low1, *late = lax.optimization_barrier((part, low1, *late))
    gathered = [swap(part, "leaf", 4), swap(part[64:], "leaf", 8), swap(part[64:], "leaf", 12)]
    node1 = swap(low1, "leaf", 2) + swap(low1, "leaf", 3)

    result, applied = expand(*late, node1, part, *gathered)

    far = swap(applied, "probe", 2)
    beside = swap(applied, "probe", 1)
    first = around(gram([applied, beside], applied), 4)
    far, *first = lax.optimization_barrier((far, *first))
    across = swap(far, "probe", 1)
    second = around(gram([far, across], applied), 4)
    blocks = around(cut_y(first, second), 16)
    blocks = around(cut_z(blocks), 1)
    total = (blocks[0] + blocks[1]) + (blocks[2] + blocks[3])
    return result, total / (leaf_points * lax.axis_size("leaf"))


def solution(mesh):
    return jax.shard_map(
        local,
        mesh=mesh,
        in_specs=(
            P("leaf", None),
            P("leaf", None, None),
            P(None, "leaf", None),
            P(None, "leaf", None),
            P("leaf", "probe"),
        ),
        out_specs=(P("leaf", "probe"), P("leaf", "probe")),
        check_vma=False,
    )
```

```python
import functools

import jax
import jax.numpy as jnp
from jax import lax
from jax.experimental import pallas as pl
from jax.experimental.pallas import tpu as pltpu
from jax.sharding import PartitionSpec as P

HIGH = lax.Precision.HIGH
F32 = jnp.float32
LIMIT = 40 * 2**20
MOST = 52 * 2**20


def swap(value, axis, mask):
    pairs = [(source, source ^ mask) for source in range(lax.axis_size(axis))]
    return lax.ppermute(value, axis, pairs)


def split(value):
    top = value.astype(jnp.bfloat16)
    return top, (value - top.astype(F32)).astype(jnp.bfloat16)


def dot3(left, right, dims):
    dot = functools.partial(
        lax.dot_general, dimension_numbers=(dims, ((), ())), preferred_element_type=F32
    )
    return dot(left[0], right[0]) + (dot(left[0], right[1]) + dot(left[1], right[0]))


ROWS = ((0,), (0,))
MATMUL = ((1,), (0,))


def whole(shape):
    return pl.BlockSpec(shape, lambda *_: (0,) * len(shape))


def shapes(*dims):
    return [jax.ShapeDtypeStruct(d, F32) for d in dims]


def call(
    body, outs, specs, operands, scratch=(), flops=0, grid=(1,), out_specs=None, limit=LIMIT
):
    moved = sum(o.size * 4 for o in operands) + sum(o.size * 4 for o in outs)
    return pl.pallas_call(
        body,
        out_shape=outs,
        grid=grid,
        in_specs=specs,
        out_specs=[whole(o.shape) for o in outs] if out_specs is None else out_specs,
        scratch_shapes=list(scratch),
        compiler_params=pltpu.CompilerParams(vmem_limit_bytes=limit),
        cost_estimate=pl.CostEstimate(flops=flops, bytes_accessed=moved, transcendentals=0),
    )(*operands)


def place():
    leaf = lax.axis_index("leaf")
    return leaf >> 4, (leaf >> 2) & 3, leaf & 3


def project_high(columns, probes):
    def body(c_ref, p_ref, keep, one, two, three, total):
        _, x, _ = place()
        right = split(p_ref[...])
        for level in range(3):
            total[level] = dot3(split(c_ref[level]), right, ROWS)
        for part, out in ((1, one), (2, two), (3, three)):
            base = 0 if part == 1 else 64
            if part > 1:
                half = ((x ^ part) & 1) * 64
                out[:64] = total[0, pl.ds(pl.multiple_of(half, 64), 64)]
            row = pl.multiple_of((x ^ part) * 32, 32)
            out[base:base + 32] = total[1, pl.ds(row, 32)]
            out[base + 32:base + 64] = total[2, pl.ds(row, 32)]
        row = pl.multiple_of(x * 32, 32)
        keep[:32] = total[1, pl.ds(row, 32)]
        keep[32:] = total[2, pl.ds(row, 32)]

    _, points, rank = columns.shape
    wide = probes.shape[1]
    return call(
        body,
        shapes((64, wide), (64, wide), (128, wide), (128, wide)),
        [pl.BlockSpec((3, points, rank), lambda _: (1, 0, 0)), whole(probes.shape)],
        [columns, probes],
        [pltpu.VMEM((3, rank, wide), F32)],
        flops=18 * points * rank * wide,
        limit=MOST,
    )


def project_low(columns, probes):
    def body(c_ref, p_ref, *outs):
        right = split(p_ref[...])
        for level, out in enumerate(outs):
            out[...] = dot3(split(c_ref[level]), right, ROWS)

    _, points, rank = columns.shape
    wide = probes.shape[1]
    return call(
        body,
        shapes(*[(rank, wide)] * 3),
        [pl.BlockSpec((3, points, rank), lambda _: (0, 0, 0)), whole(probes.shape)],
        [columns, probes],
        flops=18 * points * rank * wide,
        limit=LIMIT,
    )


LATE = (0, 3, 4, 5)


def prepare(near, rows, one, one_more, two):
    def body(n_ref, u_ref, o_ref, m_ref, t_ref, out, high, low):
        early = jnp.concatenate([u_ref[1], u_ref[2]], axis=1)
        nodes = jnp.concatenate([o_ref[...] + m_ref[...], t_ref[...]], axis=0)
        out[...] = n_ref[...] + dot3(split(early), split(nodes), MATMUL)
        high[...], low[...] = split(jnp.concatenate([u_ref[t] for t in LATE], axis=1))

    levels, points, rank = rows.shape
    wide = near.shape[1]
    tile = 256

    def tiled(width):
        return pl.BlockSpec((tile, width), lambda i: (i, 0))

    late = jax.ShapeDtypeStruct((points, len(LATE) * rank), jnp.bfloat16)
    return call(
        body,
        shapes(near.shape) + [late, late],
        [
            tiled(wide),
            pl.BlockSpec((levels, tile, rank), lambda i: (0, i, 0)),
            whole(one.shape),
            whole(one_more.shape),
            whole(two.shape),
        ],
        [near, rows, one, one_more, two],
        flops=12 * rank * points * wide,
        grid=(points // tile,),
        out_specs=[tiled(wide), tiled(len(LATE) * rank), tiled(len(LATE) * rank)],
    )


def expand(base, rows_high, rows_low, zero, part, part1, part2, part3):
    def body(b_ref, h_ref, l_ref, z_ref, q0, q1, q2, q3, out, held, total):
        _, x, _ = place()
        total[0:128] = z_ref[...]
        for k, ref in ((0, q0), (1, q1)):
            total[pl.ds(pl.multiple_of(128 + ((x ^ k) & 1) * 64, 64), 64)] = ref[:64]
        for k, ref in ((0, q0), (1, q1), (2, q2), (3, q3)):
            base = 64 if k < 2 else 0
            row = pl.multiple_of((x ^ k) * 32, 32)
            total[pl.ds(256 + row, 32)] = ref[base:base + 32]
            total[pl.ds(384 + row, 32)] = ref[base + 32:base + 64]
        left = h_ref[...], l_ref[...]
        held[...] = b_ref[...] + dot3(left, split(total[...]), MATMUL)
        out[...] = held[...]

    points, wide = base.shape
    depth = rows_high.shape[1]
    given = [base, rows_high, rows_low, zero, part, part1, part2, part3]
    return call(
        body,
        shapes(base.shape, base.shape),
        [whole(g.shape) for g in given],
        given,
        [pltpu.VMEM((depth, wide), F32)],
        flops=6 * depth * points * wide,
    )


def gram(others, applied):
    wide = applied.shape[1]
    given = [applied] if others[0] is applied else [applied, others[0]]
    given = given + [others[1]]

    def body(*refs):
        (a_ref, first), second = (refs[0], refs[len(given) - 2]), refs[len(given) - 1]
        outs, total = refs[len(given):-1], refs[-1]
        _, x, _ = place()
        right = split(a_ref[...])
        left = right if first is a_ref else split(first[...])
        total[0] = dot3(left, right, ROWS)
        total[1] = dot3(split(second[...]), right, ROWS)
        for k, out in enumerate(outs):
            row = pl.multiple_of((x ^ k) * (wide // 4), wide // 4)
            out[...] = total[:, pl.ds(row, wide // 4)]

    return call(
        body,
        shapes(*[(2, wide // 4, wide)] * 4),
        [whole(g.shape) for g in given],
        given,
        [pltpu.VMEM((2, wide, wide), F32)],
        flops=12 * wide * wide * applied.shape[0],
    )


def cut_y(near, far):
    _, rows, wide = near[0].shape

    def body(*refs):
        ins, outs, total = refs[:8], refs[8:12], refs[12]
        y, _, _ = place()
        probe = lax.axis_index("probe")
        total[:2] = (ins[0][...] + ins[1][...]) + (ins[2][...] + ins[3][...])
        total[2:] = (ins[4][...] + ins[5][...]) + (ins[6][...] + ins[7][...])
        for k, out in enumerate(outs):
            out[...] = total[probe ^ y ^ k]

    ins = [*near, *far]
    return call(
        body,
        shapes(*[(rows, wide)] * 4),
        [whole(i.shape) for i in ins],
        ins,
        [pltpu.VMEM((4, rows, wide), F32)],
    )


def cut_z(ins, shift):
    rows, wide = ins[0].shape
    half = rows // 2

    def body(*refs):
        *given, keep, give, total = refs
        _, _, z = place()
        side = (z >> shift) & 1
        total[...] = functools.reduce(jnp.add, [ref[...] for ref in given])
        keep[...] = total[pl.ds(pl.multiple_of(side * half, half), half)]
        give[...] = total[pl.ds(pl.multiple_of((1 - side) * half, half), half)]

    return call(
        body,
        shapes(*[(half, wide)] * 2),
        [whole(i.shape) for i in ins],
        list(ins),
        [pltpu.VMEM((rows, wide), F32)],
    )


def around(parts, scale):
    return [parts[0]] + [swap(parts[k], "leaf", k * scale) for k in (1, 2, 3)]


def local(leaf_blocks, block_mask, row_factor_stack, column_factor_stack, probes):
    leaf_points = leaf_blocks.shape[1]
    side = block_mask.shape[1]
    span = leaf_points // side

    weights = block_mask[0].astype(F32)
    masked = (
        leaf_blocks.reshape(side, span, side, span) * weights[:, None, :, None]
    ).reshape(leaf_points, leaf_points)
    near = jnp.dot(masked, probes, precision=HIGH, preferred_element_type=F32)

    keep, *sent = project_high(column_factor_stack, probes)
    _, one, two, three = around([keep, *sent], 4)
    low0, low1, low2 = project_low(column_factor_stack, probes)
    low2 = low2 + swap(low2, "leaf", 1)
    part3 = two[:64] + three[:64]
    upper = keep + one + two[64:] + three[64:]
    part4 = swap(upper[:32], "leaf", 16)
    five = upper[32:]
    part5 = swap(five, "leaf", 32) + swap(five, "leaf", 48)
    part = jnp.concatenate([part3, part4, part5])
    low2 = low2 + swap(low2, "leaf", 3)
    node2 = swap(low2, "leaf", 4)
    part, low1 = lax.optimization_barrier((part, low1))
    part = part + swap(part, "leaf", 1)
    node1 = swap(low1, "leaf", 3)
    part, node1, near = lax.optimization_barrier((part, node1, near))
    part = part + swap(part, "leaf", 3)
    node1_more = swap(node1, "leaf", 1)
    part, low0 = lax.optimization_barrier((part, low0))
    gathered = [swap(part, "leaf", 4), swap(part[64:], "leaf", 8), swap(part[64:], "leaf", 12)]
    node0 = swap(low0, "leaf", 1)
    late = prepare(near, row_factor_stack, node1, node1_more, node2)
    result, applied = expand(*late, node0, part, *gathered)

    far = swap(applied, "probe", 2)
    beside = swap(applied, "probe", 1)
    first = around(gram([applied, beside], applied), 4)
    far, *first = lax.optimization_barrier((far, *first))
    across = swap(far, "probe", 1)
    second = around(gram([far, across], applied), 4)
    blocks = around(cut_y(first, second), 16)
    keep, give = cut_z(blocks, 1)
    keep, give = cut_z([keep, swap(give, "leaf", 3)], 0)
    total = keep + swap(give, "leaf", 1)
    return result, total / (leaf_points * lax.axis_size("leaf"))


def solution(mesh):
    return jax.shard_map(
        local,
        mesh=mesh,
        in_specs=(
            P("leaf", None),
            P("leaf", None, None),
            P(None, "leaf", None),
            P(None, "leaf", None),
            P("leaf", "probe"),
        ),
        out_specs=(P("leaf", "probe"), P("leaf", "probe")),
        check_vma=False,
    )
```

```python
import functools

import jax
import jax.numpy as jnp
from jax import lax
from jax.experimental import pallas as pl
from jax.experimental.pallas import tpu as pltpu
from jax.sharding import PartitionSpec as P

HIGH = lax.Precision.HIGH
F32 = jnp.float32
LIMIT = 40 * 2**20
MOST = 53 * 2**20


def swap(value, axis, mask):
    pairs = [(source, source ^ mask) for source in range(lax.axis_size(axis))]
    return lax.ppermute(value, axis, pairs)


def split(value):
    top = value.astype(jnp.bfloat16)
    return top, (value - top.astype(F32)).astype(jnp.bfloat16)


def dot3(left, right, dims):
    dot = functools.partial(
        lax.dot_general, dimension_numbers=(dims, ((), ())), preferred_element_type=F32
    )
    return dot(left[0], right[0]) + (dot(left[0], right[1]) + dot(left[1], right[0]))


ROWS = ((0,), (0,))
MATMUL = ((1,), (0,))


def whole(shape):
    return pl.BlockSpec(shape, lambda *_: (0,) * len(shape))


def shapes(*dims):
    return [jax.ShapeDtypeStruct(d, F32) for d in dims]


def call(
    body, outs, specs, operands, scratch=(), flops=0, grid=(1,), out_specs=None, limit=LIMIT
):
    moved = sum(o.size * 4 for o in operands) + sum(o.size * 4 for o in outs)
    return pl.pallas_call(
        body,
        out_shape=outs,
        grid=grid,
        in_specs=specs,
        out_specs=[whole(o.shape) for o in outs] if out_specs is None else out_specs,
        scratch_shapes=list(scratch),
        compiler_params=pltpu.CompilerParams(vmem_limit_bytes=limit),
        cost_estimate=pl.CostEstimate(flops=flops, bytes_accessed=moved, transcendentals=0),
    )(*operands)


def place():
    leaf = lax.axis_index("leaf")
    return leaf >> 4, (leaf >> 2) & 3, leaf & 3


CUTS = 4


def project(columns, probes, first, outs, emit):
    _, points, rank = columns.shape
    wide = probes.shape[1]
    piece = points // CUTS

    def body(c_hbm, p_hbm, *refs):
        *results, held, given, total, sems = refs
        copies = [
            pltpu.make_async_copy(
                p_hbm.at[pl.ds(i * piece, piece)], given.at[pl.ds(i * piece, piece)], sems.at[0, i]
            )
            for i in range(CUTS)
        ]
        for level in range(3):
            for i in range(CUTS):
                copies.append(
                    pltpu.make_async_copy(
                        c_hbm.at[first + level, pl.ds(i * piece, piece)],
                        held.at[level, pl.ds(i * piece, piece)],
                        sems.at[level + 1, i],
                    )
                )
        for copy in copies:
            copy.start()
        for copy in copies[:CUTS]:
            copy.wait()
        right = split(given[...])
        for level in range(3):
            for copy in copies[(level + 1) * CUTS:(level + 2) * CUTS]:
                copy.wait()
            total[level] = dot3(split(held[level]), right, ROWS)
        emit(total, *results)

    return call(
        body,
        outs,
        [pl.BlockSpec(memory_space=pltpu.HBM)] * 2,
        [columns, probes],
        [
            pltpu.VMEM((3, points, rank), F32),
            pltpu.VMEM((points, wide), F32),
            pltpu.VMEM((3, rank, wide), F32),
            pltpu.SemaphoreType.DMA((4, CUTS)),
        ],
        flops=18 * points * rank * wide,
        limit=MOST,
    )


def project_high(columns, probes):
    def emit(total, keep, one, two, three):
        _, x, _ = place()
        for part, out in ((1, one), (2, two), (3, three)):
            base = 0 if part == 1 else 64
            if part > 1:
                half = ((x ^ part) & 1) * 64
                out[:64] = total[0, pl.ds(pl.multiple_of(half, 64), 64)]
            row = pl.multiple_of((x ^ part) * 32, 32)
            out[base:base + 32] = total[1, pl.ds(row, 32)]
            out[base + 32:base + 64] = total[2, pl.ds(row, 32)]
        row = pl.multiple_of(x * 32, 32)
        keep[:32] = total[1, pl.ds(row, 32)]
        keep[32:] = total[2, pl.ds(row, 32)]

    wide = probes.shape[1]
    outs = shapes((64, wide), (64, wide), (128, wide), (128, wide))
    return project(columns, probes, 3, outs, emit)


def project_low(columns, probes):
    def emit(total, *outs):
        for level, out in enumerate(outs):
            out[...] = total[level]

    outs = shapes(*[(columns.shape[2], probes.shape[1])] * 3)
    return project(columns, probes, 0, outs, emit)


LATE = (0, 3, 4, 5)


def prepare(near, rows, one, one_more, two):
    def body(n_ref, u_ref, o_ref, m_ref, t_ref, out, high, low):
        early = jnp.concatenate([u_ref[1], u_ref[2]], axis=1)
        nodes = jnp.concatenate([o_ref[...] + m_ref[...], t_ref[...]], axis=0)
        out[...] = n_ref[...] + dot3(split(early), split(nodes), MATMUL)
        high[...], low[...] = split(jnp.concatenate([u_ref[t] for t in LATE], axis=1))

    levels, points, rank = rows.shape
    wide = near.shape[1]
    tile = 256

    def tiled(width):
        return pl.BlockSpec((tile, width), lambda i: (i, 0))

    late = jax.ShapeDtypeStruct((points, len(LATE) * rank), jnp.bfloat16)
    return call(
        body,
        shapes(near.shape) + [late, late],
        [
            tiled(wide),
            pl.BlockSpec((levels, tile, rank), lambda i: (0, i, 0)),
            whole(one.shape),
            whole(one_more.shape),
            whole(two.shape),
        ],
        [near, rows, one, one_more, two],
        flops=12 * rank * points * wide,
        grid=(points // tile,),
        out_specs=[tiled(wide), tiled(len(LATE) * rank), tiled(len(LATE) * rank)],
    )


def expand(base, rows_high, rows_low, zero, part, part1, part2, part3):
    def body(b_ref, h_ref, l_ref, z_ref, q0, q1, q2, q3, out, held, total):
        _, x, _ = place()
        total[0:128] = z_ref[...]
        for k, ref in ((0, q0), (1, q1)):
            total[pl.ds(pl.multiple_of(128 + ((x ^ k) & 1) * 64, 64), 64)] = ref[:64]
        for k, ref in ((0, q0), (1, q1), (2, q2), (3, q3)):
            base = 64 if k < 2 else 0
            row = pl.multiple_of((x ^ k) * 32, 32)
            total[pl.ds(256 + row, 32)] = ref[base:base + 32]
            total[pl.ds(384 + row, 32)] = ref[base + 32:base + 64]
        left = h_ref[...], l_ref[...]
        held[...] = b_ref[...] + dot3(left, split(total[...]), MATMUL)
        out[...] = held[...]

    points, wide = base.shape
    depth = rows_high.shape[1]
    given = [base, rows_high, rows_low, zero, part, part1, part2, part3]
    return call(
        body,
        shapes(base.shape, base.shape),
        [whole(g.shape) for g in given],
        given,
        [pltpu.VMEM((depth, wide), F32)],
        flops=6 * depth * points * wide,
    )


def gram(others, applied):
    wide = applied.shape[1]
    given = [applied] if others[0] is applied else [applied, others[0]]
    given = given + [others[1]]

    def body(*refs):
        (a_ref, first), second = (refs[0], refs[len(given) - 2]), refs[len(given) - 1]
        outs, total = refs[len(given):-1], refs[-1]
        _, x, _ = place()
        right = split(a_ref[...])
        left = right if first is a_ref else split(first[...])
        total[0] = dot3(left, right, ROWS)
        total[1] = dot3(split(second[...]), right, ROWS)
        for k, out in enumerate(outs):
            row = pl.multiple_of((x ^ k) * (wide // 4), wide // 4)
            out[...] = total[:, pl.ds(row, wide // 4)]

    return call(
        body,
        shapes(*[(2, wide // 4, wide)] * 4),
        [whole(g.shape) for g in given],
        given,
        [pltpu.VMEM((2, wide, wide), F32)],
        flops=12 * wide * wide * applied.shape[0],
    )


def cut_y(near, far):
    _, rows, wide = near[0].shape

    def body(*refs):
        ins, outs, total = refs[:8], refs[8:12], refs[12]
        y, _, _ = place()
        probe = lax.axis_index("probe")
        total[:2] = (ins[0][...] + ins[1][...]) + (ins[2][...] + ins[3][...])
        total[2:] = (ins[4][...] + ins[5][...]) + (ins[6][...] + ins[7][...])
        for k, out in enumerate(outs):
            out[...] = total[probe ^ y ^ k]

    ins = [*near, *far]
    return call(
        body,
        shapes(*[(rows, wide)] * 4),
        [whole(i.shape) for i in ins],
        ins,
        [pltpu.VMEM((4, rows, wide), F32)],
    )


def cut_z(ins, shift):
    rows, wide = ins[0].shape
    half = rows // 2

    def body(*refs):
        *given, keep, give, total = refs
        _, _, z = place()
        side = (z >> shift) & 1
        total[...] = functools.reduce(jnp.add, [ref[...] for ref in given])
        keep[...] = total[pl.ds(pl.multiple_of(side * half, half), half)]
        give[...] = total[pl.ds(pl.multiple_of((1 - side) * half, half), half)]

    return call(
        body,
        shapes(*[(half, wide)] * 2),
        [whole(i.shape) for i in ins],
        list(ins),
        [pltpu.VMEM((rows, wide), F32)],
    )


def around(parts, scale):
    return [parts[0]] + [swap(parts[k], "leaf", k * scale) for k in (1, 2, 3)]


def near_product(leaf_blocks, block_mask, probes):
    leaf_points = leaf_blocks.shape[1]
    side = block_mask.shape[1]
    span = leaf_points // side

    weights = block_mask[0].astype(F32)
    masked = (
        leaf_blocks.reshape(side, span, side, span) * weights[:, None, :, None]
    ).reshape(leaf_points, leaf_points)
    return jnp.dot(masked, probes, precision=HIGH, preferred_element_type=F32)


def local(leaf_blocks, block_mask, row_factor_stack, column_factor_stack, probes):
    leaf_points = leaf_blocks.shape[1]
    keep, *sent = project_high(column_factor_stack, probes)
    _, one, two, three = around([keep, *sent], 4)
    low0, low1, low2 = project_low(column_factor_stack, probes)
    low2 = low2 + swap(low2, "leaf", 1)
    part3 = two[:64] + three[:64]
    upper = keep + one + two[64:] + three[64:]
    part4 = swap(upper[:32], "leaf", 16)
    five = upper[32:]
    part5 = swap(five, "leaf", 32) + swap(five, "leaf", 48)
    part = jnp.concatenate([part3, part4, part5])
    low2 = low2 + swap(low2, "leaf", 3)
    node2 = swap(low2, "leaf", 4)
    part, blocks, low1 = lax.optimization_barrier((part, leaf_blocks, low1))
    near = near_product(blocks, block_mask, probes)
    part = part + swap(part, "leaf", 1)
    near, low1 = lax.optimization_barrier((near, low1))
    node1 = swap(low1, "leaf", 3)
    part, near = lax.optimization_barrier((part, near))
    part = part + swap(part, "leaf", 3)
    node1_more = swap(node1, "leaf", 1)
    part, low0 = lax.optimization_barrier((part, low0))
    gathered = [swap(part, "leaf", 4), swap(part[64:], "leaf", 8), swap(part[64:], "leaf", 12)]
    node0 = swap(low0, "leaf", 1)
    late = prepare(near, row_factor_stack, node1, node1_more, node2)
    result, applied = expand(*late, node0, part, *gathered)

    far = swap(applied, "probe", 2)
    beside = swap(applied, "probe", 1)
    first = around(gram([applied, beside], applied), 4)
    far, *first = lax.optimization_barrier((far, *first))
    across = swap(far, "probe", 1)
    second = around(gram([far, across], applied), 4)
    blocks = around(cut_y(first, second), 16)
    keep, give = cut_z(blocks, 1)
    keep, give = cut_z([keep, swap(give, "leaf", 3)], 0)
    total = keep + swap(give, "leaf", 1)
    return result, total / (leaf_points * lax.axis_size("leaf"))


def solution(mesh):
    return jax.shard_map(
        local,
        mesh=mesh,
        in_specs=(
            P("leaf", None),
            P("leaf", None, None),
            P(None, "leaf", None),
            P(None, "leaf", None),
            P("leaf", "probe"),
        ),
        out_specs=(P("leaf", "probe"), P("leaf", "probe")),
        check_vma=False,
    )
```

```python
import functools

import jax
import jax.numpy as jnp
from jax import lax
from jax.experimental import pallas as pl
from jax.experimental.pallas import tpu as pltpu
from jax.sharding import PartitionSpec as P

HIGH = lax.Precision.HIGH
F32 = jnp.float32
LIMIT = 40 * 2**20
MOST = 53 * 2**20


def swap(value, axis, mask):
    pairs = [(source, source ^ mask) for source in range(lax.axis_size(axis))]
    return lax.ppermute(value, axis, pairs)


def split(value):
    top = value.astype(jnp.bfloat16)
    return top, (value - top.astype(F32)).astype(jnp.bfloat16)


def dot3(left, right, dims):
    dot = functools.partial(
        lax.dot_general, dimension_numbers=(dims, ((), ())), preferred_element_type=F32
    )
    return dot(left[0], right[0]) + (dot(left[0], right[1]) + dot(left[1], right[0]))


ROWS = ((0,), (0,))
MATMUL = ((1,), (0,))


def whole(shape):
    return pl.BlockSpec(shape, lambda *_: (0,) * len(shape))


def shapes(*dims):
    return [jax.ShapeDtypeStruct(d, F32) for d in dims]


def call(
    body, outs, specs, operands, scratch=(), flops=0, grid=(1,), out_specs=None, limit=LIMIT
):
    moved = sum(o.size * 4 for o in operands) + sum(o.size * 4 for o in outs)
    return pl.pallas_call(
        body,
        out_shape=outs,
        grid=grid,
        in_specs=specs,
        out_specs=[whole(o.shape) for o in outs] if out_specs is None else out_specs,
        scratch_shapes=list(scratch),
        compiler_params=pltpu.CompilerParams(vmem_limit_bytes=limit),
        cost_estimate=pl.CostEstimate(flops=flops, bytes_accessed=moved, transcendentals=0),
    )(*operands)


def place():
    leaf = lax.axis_index("leaf")
    return leaf >> 4, (leaf >> 2) & 3, leaf & 3


CUTS = 4


def project(columns, probes, first, outs, emit):
    _, points, rank = columns.shape
    wide = probes.shape[1]
    piece = points // CUTS

    def body(c_hbm, p_hbm, *refs):
        *results, held, given, total, sems = refs
        copies = [
            pltpu.make_async_copy(
                p_hbm.at[pl.ds(i * piece, piece)], given.at[pl.ds(i * piece, piece)], sems.at[0, i]
            )
            for i in range(CUTS)
        ]
        for level in range(3):
            for i in range(CUTS):
                copies.append(
                    pltpu.make_async_copy(
                        c_hbm.at[first + level, pl.ds(i * piece, piece)],
                        held.at[level, pl.ds(i * piece, piece)],
                        sems.at[level + 1, i],
                    )
                )
        for copy in copies:
            copy.start()
        for copy in copies[:CUTS]:
            copy.wait()
        right = split(given[...])
        for level in range(3):
            for copy in copies[(level + 1) * CUTS:(level + 2) * CUTS]:
                copy.wait()
            total[level] = dot3(split(held[level]), right, ROWS)
        emit(total, *results)

    return call(
        body,
        outs,
        [pl.BlockSpec(memory_space=pltpu.HBM)] * 2,
        [columns, probes],
        [
            pltpu.VMEM((3, points, rank), F32),
            pltpu.VMEM((points, wide), F32),
            pltpu.VMEM((3, rank, wide), F32),
            pltpu.SemaphoreType.DMA((4, CUTS)),
        ],
        flops=18 * points * rank * wide,
        limit=MOST,
    )


def project_high(columns, probes):
    def emit(total, keep, one, two, three):
        _, x, _ = place()
        for part, out in ((1, one), (2, two), (3, three)):
            base = 0 if part == 1 else 64
            if part > 1:
                half = ((x ^ part) & 1) * 64
                out[:64] = total[0, pl.ds(pl.multiple_of(half, 64), 64)]
            row = pl.multiple_of((x ^ part) * 32, 32)
            out[base:base + 32] = total[1, pl.ds(row, 32)]
            out[base + 32:base + 64] = total[2, pl.ds(row, 32)]
        row = pl.multiple_of(x * 32, 32)
        keep[:32] = total[1, pl.ds(row, 32)]
        keep[32:] = total[2, pl.ds(row, 32)]

    wide = probes.shape[1]
    outs = shapes((64, wide), (64, wide), (128, wide), (128, wide))
    return project(columns, probes, 3, outs, emit)


def project_low(columns, probes):
    def emit(total, *outs):
        for level, out in enumerate(outs):
            out[...] = total[level]

    outs = shapes(*[(columns.shape[2], probes.shape[1])] * 3)
    return project(columns, probes, 0, outs, emit)


LATE = (0, 3, 4, 5)


def prepare(near, rows, one, one_more, two):
    def body(n_ref, u_ref, o_ref, m_ref, t_ref, out, high, low):
        early = jnp.concatenate([u_ref[1], u_ref[2]], axis=1)
        nodes = jnp.concatenate([o_ref[...] + m_ref[...], t_ref[...]], axis=0)
        out[...] = n_ref[...] + dot3(split(early), split(nodes), MATMUL)
        high[...], low[...] = split(jnp.concatenate([u_ref[t] for t in LATE], axis=1))

    levels, points, rank = rows.shape
    wide = near.shape[1]
    tile = 256

    def tiled(width):
        return pl.BlockSpec((tile, width), lambda i: (i, 0))

    late = jax.ShapeDtypeStruct((points, len(LATE) * rank), jnp.bfloat16)
    return call(
        body,
        shapes(near.shape) + [late, late],
        [
            tiled(wide),
            pl.BlockSpec((levels, tile, rank), lambda i: (0, i, 0)),
            whole(one.shape),
            whole(one_more.shape),
            whole(two.shape),
        ],
        [near, rows, one, one_more, two],
        flops=12 * rank * points * wide,
        grid=(points // tile,),
        out_specs=[tiled(wide), tiled(len(LATE) * rank), tiled(len(LATE) * rank)],
    )


def chunks(value):
    left, right = value[:, :128], value[:, 128:]
    group = lax.broadcasted_iota(jnp.int32, left.shape, 1) // 32

    def pick(*parts):
        out = parts[3]
        for k in (2, 1, 0):
            out = jnp.where(group == k, parts[k], out)
        return out

    def turn(part, groups):
        return pltpu.roll(part, groups * 32, 1) if groups else part

    even = pick(left, turn(left, 3), turn(right, 2), turn(right, 1))
    odd = pick(turn(left, 3), turn(left, 2), turn(right, 1), right)
    return even, odd


def expand(base, rows_high, rows_low, zero, part, part1, part2, part3):
    def body(b_ref, h_ref, l_ref, z_ref, q0, q1, q2, q3, out, held, even, odd, total):
        _, x, _ = place()
        total[0:128] = z_ref[...]
        for k, ref in ((0, q0), (1, q1)):
            total[pl.ds(pl.multiple_of(128 + ((x ^ k) & 1) * 64, 64), 64)] = ref[:64]
        for k, ref in ((0, q0), (1, q1), (2, q2), (3, q3)):
            base = 64 if k < 2 else 0
            row = pl.multiple_of((x ^ k) * 32, 32)
            total[pl.ds(256 + row, 32)] = ref[base:base + 32]
            total[pl.ds(384 + row, 32)] = ref[base + 32:base + 64]
        left = h_ref[...], l_ref[...]
        value = b_ref[...] + dot3(left, split(total[...]), MATMUL)
        out[...] = value
        held[...] = value
        even[...], odd[...] = chunks(value)

    points, wide = base.shape
    depth = rows_high.shape[1]
    given = [base, rows_high, rows_low, zero, part, part1, part2, part3]
    return call(
        body,
        shapes(base.shape, base.shape, (points, wide // 2), (points, wide // 2)),
        [whole(g.shape) for g in given],
        given,
        [pltpu.VMEM((depth, wide), F32)],
        flops=6 * depth * points * wide,
    )


def gram(others, applied):
    wide = applied.shape[1]
    tall = others[1].shape[1]
    part = tall // 4
    given = [applied] if others[0] is applied else [applied, others[0]]
    given = given + [others[1]]

    def body(*refs):
        (a_ref, first), second = (refs[0], refs[len(given) - 2]), refs[len(given) - 1]
        outs, total = refs[len(given):-1], refs[-1]
        _, x, _ = place()
        right = split(a_ref[...])
        left = right if first is a_ref else split(first[...])
        total[0] = dot3(left, right, ROWS)
        total[1] = dot3(split(second[...]), right, ROWS)
        for k, out in enumerate(outs):
            out[...] = total[:, pl.ds(pl.multiple_of((x ^ k) * part, part), part)]

    return call(
        body,
        shapes(*[(2, part, wide)] * 4),
        [whole(g.shape) for g in given],
        given,
        [pltpu.VMEM((2, tall, wide), F32)],
        flops=12 * tall * wide * applied.shape[0],
    )


def cut_y(near, far_even, far_odd):
    _, rows, wide = near[0].shape
    half = rows // 2

    def body(*refs):
        ins, outs, total = refs[:12], refs[12:16], refs[16]
        y, _, _ = place()
        probe = lax.axis_index("probe")

        def add(four):
            return (four[0][...] + four[1][...]) + (four[2][...] + four[3][...])

        total[:2] = add(ins[:4])
        total[2:, :half] = add(ins[4:8])
        total[2:, half:] = add(ins[8:])
        for k, out in enumerate(outs):
            out[...] = total[probe ^ y ^ k]

    ins = [*near, *far_even, *far_odd]
    return call(
        body,
        shapes(*[(rows, wide)] * 4),
        [whole(i.shape) for i in ins],
        ins,
        [pltpu.VMEM((4, rows, wide), F32)],
    )


def cut_z(ins, shift):
    rows, wide = ins[0].shape
    half = rows // 2

    def body(*refs):
        *given, keep, give, total = refs
        _, _, z = place()
        side = (z >> shift) & 1
        total[...] = functools.reduce(jnp.add, [ref[...] for ref in given])
        keep[...] = total[pl.ds(pl.multiple_of(side * half, half), half)]
        give[...] = total[pl.ds(pl.multiple_of((1 - side) * half, half), half)]

    return call(
        body,
        shapes(*[(half, wide)] * 2),
        [whole(i.shape) for i in ins],
        list(ins),
        [pltpu.VMEM((rows, wide), F32)],
    )


def around(parts, scale):
    return [parts[0]] + [swap(parts[k], "leaf", k * scale) for k in (1, 2, 3)]


def near_product(leaf_blocks, block_mask, probes):
    leaf_points = leaf_blocks.shape[1]
    side = block_mask.shape[1]
    span = leaf_points // side

    weights = block_mask[0].astype(F32)
    masked = (
        leaf_blocks.reshape(side, span, side, span) * weights[:, None, :, None]
    ).reshape(leaf_points, leaf_points)
    return jnp.dot(masked, probes, precision=HIGH, preferred_element_type=F32)


def local(leaf_blocks, block_mask, row_factor_stack, column_factor_stack, probes):
    leaf_points = leaf_blocks.shape[1]
    keep, *sent = project_high(column_factor_stack, probes)
    _, one, two, three = around([keep, *sent], 4)
    low0, low1, low2 = project_low(column_factor_stack, probes)
    low2 = low2 + swap(low2, "leaf", 1)
    part3 = two[:64] + three[:64]
    upper = keep + one + two[64:] + three[64:]
    part4 = swap(upper[:32], "leaf", 16)
    five = upper[32:]
    part5 = swap(five, "leaf", 32) + swap(five, "leaf", 48)
    part = jnp.concatenate([part3, part4, part5])
    low2 = low2 + swap(low2, "leaf", 3)
    node2 = swap(low2, "leaf", 4)
    part, blocks, low1 = lax.optimization_barrier((part, leaf_blocks, low1))
    near = near_product(blocks, block_mask, probes)
    part = part + swap(part, "leaf", 1)
    near, low1 = lax.optimization_barrier((near, low1))
    node1 = swap(low1, "leaf", 3)
    part, near = lax.optimization_barrier((part, near))
    part = part + swap(part, "leaf", 3)
    node1_more = swap(node1, "leaf", 1)
    part, low0 = lax.optimization_barrier((part, low0))
    gathered = [swap(part, "leaf", 4), swap(part[64:], "leaf", 8), swap(part[64:], "leaf", 12)]
    node0 = swap(low0, "leaf", 1)
    late = prepare(near, row_factor_stack, node1, node1_more, node2)
    result, applied, even, odd = expand(*late, node0, part, *gathered)

    even = swap(even, "probe", 2)
    odd = swap(odd, "probe", 2)
    beside = swap(applied, "probe", 1)
    first = around(gram([applied, beside], applied), 4)
    even, *first = lax.optimization_barrier((even, *first))
    second = around(gram([even, swap(even, "probe", 1)], applied), 4)
    odd, *second = lax.optimization_barrier((odd, *second))
    third = around(gram([odd, swap(odd, "probe", 1)], applied), 4)
    blocks = around(cut_y(first, second, third), 16)
    keep, give = cut_z(blocks, 1)
    keep, give = cut_z([keep, swap(give, "leaf", 3)], 0)
    total = keep + swap(give, "leaf", 1)
    return result, total / (leaf_points * lax.axis_size("leaf"))


def solution(mesh):
    return jax.shard_map(
        local,
        mesh=mesh,
        in_specs=(
            P("leaf", None),
            P("leaf", None, None),
            P(None, "leaf", None),
            P(None, "leaf", None),
            P("leaf", "probe"),
        ),
        out_specs=(P("leaf", "probe"), P("leaf", "probe")),
        check_vma=False,
    )
```

```python
import functools

import jax
import jax.numpy as jnp
from jax import lax
from jax.experimental import pallas as pl
from jax.experimental.pallas import tpu as pltpu
from jax.sharding import PartitionSpec as P

HIGH = lax.Precision.HIGH
F32 = jnp.float32
LIMIT = 40 * 2**20
MOST = 53 * 2**20


def swap(value, axis, mask):
    pairs = [(source, source ^ mask) for source in range(lax.axis_size(axis))]
    return lax.ppermute(value, axis, pairs)


def split(value):
    top = value.astype(jnp.bfloat16)
    return top, (value - top.astype(F32)).astype(jnp.bfloat16)


def dot3(left, right, dims):
    dot = functools.partial(
        lax.dot_general, dimension_numbers=(dims, ((), ())), preferred_element_type=F32
    )
    return dot(left[0], right[0]) + (dot(left[0], right[1]) + dot(left[1], right[0]))


ROWS = ((0,), (0,))
MATMUL = ((1,), (0,))


def whole(shape):
    return pl.BlockSpec(shape, lambda *_: (0,) * len(shape))


def shapes(*dims):
    return [jax.ShapeDtypeStruct(d, F32) for d in dims]


def call(
    body, outs, specs, operands, scratch=(), flops=0, grid=(1,), out_specs=None, limit=LIMIT
):
    moved = sum(o.size * 4 for o in operands) + sum(o.size * 4 for o in outs)
    return pl.pallas_call(
        body,
        out_shape=outs,
        grid=grid,
        in_specs=specs,
        out_specs=[whole(o.shape) for o in outs] if out_specs is None else out_specs,
        scratch_shapes=list(scratch),
        compiler_params=pltpu.CompilerParams(vmem_limit_bytes=limit),
        cost_estimate=pl.CostEstimate(flops=flops, bytes_accessed=moved, transcendentals=0),
    )(*operands)


def place():
    leaf = lax.axis_index("leaf")
    return leaf >> 4, (leaf >> 2) & 3, leaf & 3


CUTS = 4


def project(columns, probes, first, outs, emit):
    _, points, rank = columns.shape
    wide = probes.shape[1]
    piece = points // CUTS

    def body(c_hbm, p_hbm, *refs):
        *results, held, given, total, sems = refs
        copies = [
            pltpu.make_async_copy(
                p_hbm.at[pl.ds(i * piece, piece)], given.at[pl.ds(i * piece, piece)], sems.at[0, i]
            )
            for i in range(CUTS)
        ]
        for level in range(3):
            for i in range(CUTS):
                copies.append(
                    pltpu.make_async_copy(
                        c_hbm.at[first + level, pl.ds(i * piece, piece)],
                        held.at[level, pl.ds(i * piece, piece)],
                        sems.at[level + 1, i],
                    )
                )
        for copy in copies:
            copy.start()
        for copy in copies[:CUTS]:
            copy.wait()
        right = split(given[...])
        for level in range(3):
            for copy in copies[(level + 1) * CUTS:(level + 2) * CUTS]:
                copy.wait()
            total[level] = dot3(split(held[level]), right, ROWS)
        emit(total, *results)

    return call(
        body,
        outs,
        [pl.BlockSpec(memory_space=pltpu.HBM)] * 2,
        [columns, probes],
        [
            pltpu.VMEM((3, points, rank), F32),
            pltpu.VMEM((points, wide), F32),
            pltpu.VMEM((3, rank, wide), F32),
            pltpu.SemaphoreType.DMA((4, CUTS)),
        ],
        flops=18 * points * rank * wide,
        limit=MOST,
    )


def project_high(columns, probes):
    def emit(total, keep, one, two, three):
        _, x, _ = place()
        for part, out in ((1, one), (2, two), (3, three)):
            base = 0 if part == 1 else 64
            if part > 1:
                half = ((x ^ part) & 1) * 64
                out[:64] = total[0, pl.ds(pl.multiple_of(half, 64), 64)]
            row = pl.multiple_of((x ^ part) * 32, 32)
            out[base:base + 32] = total[1, pl.ds(row, 32)]
            out[base + 32:base + 64] = total[2, pl.ds(row, 32)]
        row = pl.multiple_of(x * 32, 32)
        keep[:32] = total[1, pl.ds(row, 32)]
        keep[32:] = total[2, pl.ds(row, 32)]

    wide = probes.shape[1]
    outs = shapes((64, wide), (64, wide), (128, wide), (128, wide))
    return project(columns, probes, 3, outs, emit)


def project_low(columns, probes):
    def emit(total, *outs):
        for level, out in enumerate(outs):
            out[...] = total[level]

    outs = shapes(*[(columns.shape[2], probes.shape[1])] * 3)
    return project(columns, probes, 0, outs, emit)


LATE = (0, 3, 4, 5)


def prepare(near, rows, one, one_more, two):
    def body(n_ref, u_ref, o_ref, m_ref, t_ref, out, high, low):
        early = jnp.concatenate([u_ref[1], u_ref[2]], axis=1)
        nodes = jnp.concatenate([o_ref[...] + m_ref[...], t_ref[...]], axis=0)
        out[...] = n_ref[...] + dot3(split(early), split(nodes), MATMUL)
        high[...], low[...] = split(jnp.concatenate([u_ref[t] for t in LATE], axis=1))

    levels, points, rank = rows.shape
    wide = near.shape[1]
    tile = 256

    def tiled(width):
        return pl.BlockSpec((tile, width), lambda i: (i, 0))

    late = jax.ShapeDtypeStruct((points, len(LATE) * rank), jnp.bfloat16)
    return call(
        body,
        shapes(near.shape) + [late, late],
        [
            tiled(wide),
            pl.BlockSpec((levels, tile, rank), lambda i: (0, i, 0)),
            whole(one.shape),
            whole(one_more.shape),
            whole(two.shape),
        ],
        [near, rows, one, one_more, two],
        flops=12 * rank * points * wide,
        grid=(points // tile,),
        out_specs=[tiled(wide), tiled(len(LATE) * rank), tiled(len(LATE) * rank)],
    )


def chunks(value):
    left, right = value[:, :128], value[:, 128:]
    group = lax.broadcasted_iota(jnp.int32, left.shape, 1) // 32

    def pick(*parts):
        out = parts[3]
        for k in (2, 1, 0):
            out = jnp.where(group == k, parts[k], out)
        return out

    def turn(part, groups):
        return pltpu.roll(part, groups * 32, 1) if groups else part

    even = pick(left, turn(left, 3), turn(right, 2), turn(right, 1))
    odd = pick(turn(left, 3), turn(left, 2), turn(right, 1), right)
    return even, odd


def expand(base, rows_high, rows_low, zero, part, part1, part2, part3):
    def body(b_ref, h_ref, l_ref, z_ref, q0, q1, q2, q3, out, held, even, odd, total):
        _, x, _ = place()
        total[0:128] = z_ref[...]
        for k, ref in ((0, q0), (1, q1)):
            total[pl.ds(pl.multiple_of(128 + ((x ^ k) & 1) * 64, 64), 64)] = ref[:64]
        for k, ref in ((0, q0), (1, q1), (2, q2), (3, q3)):
            base = 64 if k < 2 else 0
            row = pl.multiple_of((x ^ k) * 32, 32)
            total[pl.ds(256 + row, 32)] = ref[base:base + 32]
            total[pl.ds(384 + row, 32)] = ref[base + 32:base + 64]
        left = h_ref[...], l_ref[...]
        value = b_ref[...] + dot3(left, split(total[...]), MATMUL)
        out[...] = value
        held[...] = value
        even[...], odd[...] = chunks(value)

    points, wide = base.shape
    depth = rows_high.shape[1]
    given = [base, rows_high, rows_low, zero, part, part1, part2, part3]
    return call(
        body,
        shapes(base.shape, base.shape, (points, wide // 2), (points, wide // 2)),
        [whole(g.shape) for g in given],
        given,
        [pltpu.VMEM((depth, wide), F32)],
        flops=6 * depth * points * wide,
    )


def gram(left, first, second):
    wide = first.shape[1]
    near = left is first
    tall = left.shape[1]
    part = tall // 4
    given = [first, second] if near else [first, second, left]

    def body(*refs):
        a_ref, b_ref = refs[0], refs[1]
        outs, total = refs[len(given):-1], refs[-1]
        _, x, _ = place()
        mine, beside = split(a_ref[...]), split(b_ref[...])
        if near:
            pairs = (mine, mine), (beside, mine)
        else:
            rows = split(refs[2][...])
            pairs = (rows, mine), (rows, beside)
        for k, (up, down) in enumerate(pairs):
            total[k] = dot3(up, down, ROWS)
        for k, out in enumerate(outs):
            out[...] = total[:, pl.ds(pl.multiple_of((x ^ k) * part, part), part)]

    return call(
        body,
        shapes(*[(2, part, wide)] * 4),
        [whole(g.shape) for g in given],
        given,
        [pltpu.VMEM((2, tall, wide), F32)],
        flops=12 * tall * wide * first.shape[0],
    )


def add_x(near, far_even, far_odd):
    _, rows, wide = near[0].shape
    half = rows // 2

    def body(*refs):
        ins, mine, give = refs[:12], refs[12], refs[13]

        def add(four, block):
            return (four[0][block] + four[1][block]) + (four[2][block] + four[3][block])

        for block in range(2):
            mine[block] = add(ins[:4], block)
        mine[2, :half] = add(ins[4:8], 0)
        mine[2, half:] = add(ins[8:], 0)
        give[:half] = add(ins[4:8], 1)
        give[half:] = add(ins[8:], 1)

    ins = [*near, *far_even, *far_odd]
    return call(body, shapes((3, rows, wide), (rows, wide)), [whole(i.shape) for i in ins], ins)


def cut_y(mine, got):
    blocks, rows, wide = mine.shape

    def body(mine_ref, got_ref, *refs):
        *outs, total = refs
        y, _, _ = place()
        probe = lax.axis_index("probe")
        total[:blocks] = mine_ref[...]
        total[blocks] = got_ref[...]
        for k, out in enumerate(outs):
            out[...] = total[probe ^ y ^ k]

    return call(
        body,
        shapes(*[(rows, wide)] * 4),
        [whole(mine.shape), whole(got.shape)],
        [mine, got],
        [pltpu.VMEM((blocks + 1, rows, wide), F32)],
    )


def cut_z(ins, shift):
    rows, wide = ins[0].shape
    half = rows // 2

    def body(*refs):
        *given, keep, give, total = refs
        _, _, z = place()
        side = (z >> shift) & 1
        total[...] = functools.reduce(jnp.add, [ref[...] for ref in given])
        keep[...] = total[pl.ds(pl.multiple_of(side * half, half), half)]
        give[...] = total[pl.ds(pl.multiple_of((1 - side) * half, half), half)]

    return call(
        body,
        shapes(*[(half, wide)] * 2),
        [whole(i.shape) for i in ins],
        list(ins),
        [pltpu.VMEM((rows, wide), F32)],
    )


def around(parts, scale):
    return [parts[0]] + [swap(parts[k], "leaf", k * scale) for k in (1, 2, 3)]


def near_product(leaf_blocks, block_mask, probes):
    leaf_points = leaf_blocks.shape[1]
    side = block_mask.shape[1]
    span = leaf_points // side

    weights = block_mask[0].astype(F32)
    masked = (
        leaf_blocks.reshape(side, span, side, span) * weights[:, None, :, None]
    ).reshape(leaf_points, leaf_points)
    return jnp.dot(masked, probes, precision=HIGH, preferred_element_type=F32)


def local(leaf_blocks, block_mask, row_factor_stack, column_factor_stack, probes):
    leaf_points = leaf_blocks.shape[1]
    keep, *sent = project_high(column_factor_stack, probes)
    _, one, two, three = around([keep, *sent], 4)
    low0, low1, low2 = project_low(column_factor_stack, probes)
    low2 = low2 + swap(low2, "leaf", 1)
    part3 = two[:64] + three[:64]
    upper = keep + one + two[64:] + three[64:]
    part4 = swap(upper[:32], "leaf", 16)
    five = upper[32:]
    part5 = swap(five, "leaf", 32) + swap(five, "leaf", 48)
    part = jnp.concatenate([part3, part4, part5])
    low2 = low2 + swap(low2, "leaf", 3)
    node2 = swap(low2, "leaf", 4)
    part, blocks, low1 = lax.optimization_barrier((part, leaf_blocks, low1))
    near = near_product(blocks, block_mask, probes)
    part = part + swap(part, "leaf", 1)
    near, low1 = lax.optimization_barrier((near, low1))
    node1 = swap(low1, "leaf", 3)
    part, near = lax.optimization_barrier((part, near))
    part = part + swap(part, "leaf", 3)
    node1_more = swap(node1, "leaf", 1)
    part, low0 = lax.optimization_barrier((part, low0))
    gathered = [swap(part, "leaf", 4), swap(part[64:], "leaf", 8), swap(part[64:], "leaf", 12)]
    node0 = swap(low0, "leaf", 1)
    late = prepare(near, row_factor_stack, node1, node1_more, node2)
    result, applied, even, odd = expand(*late, node0, part, *gathered)

    even = swap(even, "probe", 2)
    odd = swap(odd, "probe", 2)
    beside = swap(applied, "probe", 1)
    first = around(gram(applied, applied, beside), 4)
    even, *first = lax.optimization_barrier((even, *first))
    second = around(gram(even, applied, beside), 4)
    odd, *second = lax.optimization_barrier((odd, *second))
    third = around(gram(odd, applied, beside), 4)
    mine, give = add_x(first, second, third)
    blocks = around(cut_y(mine, swap(give, "probe", 1)), 16)
    keep, give = cut_z(blocks, 1)
    keep, give = cut_z([keep, swap(give, "leaf", 3)], 0)
    total = keep + swap(give, "leaf", 1)
    return result, total / (leaf_points * lax.axis_size("leaf"))


def solution(mesh):
    return jax.shard_map(
        local,
        mesh=mesh,
        in_specs=(
            P("leaf", None),
            P("leaf", None, None),
            P(None, "leaf", None),
            P(None, "leaf", None),
            P("leaf", "probe"),
        ),
        out_specs=(P("leaf", "probe"), P("leaf", "probe")),
        check_vma=False,
    )
```

```python
import functools

import jax
import jax.numpy as jnp
from jax import lax
from jax.experimental import pallas as pl
from jax.experimental.pallas import tpu as pltpu
from jax.sharding import PartitionSpec as P

HIGH = lax.Precision.HIGH
F32 = jnp.float32
LIMIT = 40 * 2**20
MOST = 53 * 2**20


def swap(value, axis, mask):
    pairs = [(source, source ^ mask) for source in range(lax.axis_size(axis))]
    return lax.ppermute(value, axis, pairs)


def split(value):
    top = value.astype(jnp.bfloat16)
    return top, (value - top.astype(F32)).astype(jnp.bfloat16)


def dot3(left, right, dims):
    dot = functools.partial(
        lax.dot_general, dimension_numbers=(dims, ((), ())), preferred_element_type=F32
    )
    return dot(left[0], right[0]) + (dot(left[0], right[1]) + dot(left[1], right[0]))


ROWS = ((0,), (0,))
MATMUL = ((1,), (0,))


def whole(shape):
    return pl.BlockSpec(shape, lambda *_: (0,) * len(shape))


def shapes(*dims):
    return [jax.ShapeDtypeStruct(d, F32) for d in dims]


def call(
    body, outs, specs, operands, scratch=(), flops=0, grid=(1,), out_specs=None, limit=LIMIT
):
    moved = sum(o.size * 4 for o in operands) + sum(o.size * 4 for o in outs)
    return pl.pallas_call(
        body,
        out_shape=outs,
        grid=grid,
        in_specs=specs,
        out_specs=[whole(o.shape) for o in outs] if out_specs is None else out_specs,
        scratch_shapes=list(scratch),
        compiler_params=pltpu.CompilerParams(vmem_limit_bytes=limit),
        cost_estimate=pl.CostEstimate(flops=flops, bytes_accessed=moved, transcendentals=0),
    )(*operands)


def place():
    leaf = lax.axis_index("leaf")
    return leaf >> 4, (leaf >> 2) & 3, leaf & 3


CUTS = 4


def project(columns, probes, first, outs, emit):
    _, points, rank = columns.shape
    wide = probes.shape[1]
    piece = points // CUTS

    def body(c_hbm, p_hbm, *refs):
        *results, held, given, total, sems = refs
        copies = [
            pltpu.make_async_copy(
                p_hbm.at[pl.ds(i * piece, piece)], given.at[pl.ds(i * piece, piece)], sems.at[0, i]
            )
            for i in range(CUTS)
        ]
        for level in range(3):
            for i in range(CUTS):
                copies.append(
                    pltpu.make_async_copy(
                        c_hbm.at[first + level, pl.ds(i * piece, piece)],
                        held.at[level, pl.ds(i * piece, piece)],
                        sems.at[level + 1, i],
                    )
                )
        for copy in copies:
            copy.start()
        for copy in copies[:CUTS]:
            copy.wait()
        right = split(given[...])
        for level in range(3):
            for copy in copies[(level + 1) * CUTS:(level + 2) * CUTS]:
                copy.wait()
            total[level] = dot3(split(held[level]), right, ROWS)
        emit(total, *results)

    return call(
        body,
        outs,
        [pl.BlockSpec(memory_space=pltpu.HBM)] * 2,
        [columns, probes],
        [
            pltpu.VMEM((3, points, rank), F32),
            pltpu.VMEM((points, wide), F32),
            pltpu.VMEM((3, rank, wide), F32),
            pltpu.SemaphoreType.DMA((4, CUTS)),
        ],
        flops=18 * points * rank * wide,
        limit=MOST,
    )


def project_high(columns, probes):
    def emit(total, keep, one, two, three):
        _, x, _ = place()
        for part, out in ((1, one), (2, two), (3, three)):
            base = 0 if part == 1 else 64
            if part > 1:
                half = ((x ^ part) & 1) * 64
                out[:64] = total[0, pl.ds(pl.multiple_of(half, 64), 64)]
            row = pl.multiple_of((x ^ part) * 32, 32)
            out[base:base + 32] = total[1, pl.ds(row, 32)]
            out[base + 32:base + 64] = total[2, pl.ds(row, 32)]
        row = pl.multiple_of(x * 32, 32)
        keep[:32] = total[1, pl.ds(row, 32)]
        keep[32:] = total[2, pl.ds(row, 32)]

    wide = probes.shape[1]
    outs = shapes((64, wide), (64, wide), (128, wide), (128, wide))
    return project(columns, probes, 3, outs, emit)


def project_low(columns, probes):
    def emit(total, *outs):
        for level, out in enumerate(outs):
            out[...] = total[level]

    outs = shapes(*[(columns.shape[2], probes.shape[1])] * 3)
    return project(columns, probes, 0, outs, emit)


LATE = (0, 1, 3, 4, 5)


def prepare(near, rows, two):
    def body(n_ref, u_ref, t_ref, out, high, low):
        out[...] = n_ref[...] + dot3(split(u_ref[2]), split(t_ref[...]), MATMUL)
        high[...], low[...] = split(jnp.concatenate([u_ref[t] for t in LATE], axis=1))

    levels, points, rank = rows.shape
    wide = near.shape[1]
    tile = 256

    def tiled(width):
        return pl.BlockSpec((tile, width), lambda i: (i, 0))

    late = jax.ShapeDtypeStruct((points, len(LATE) * rank), jnp.bfloat16)
    return call(
        body,
        shapes(near.shape) + [late, late],
        [
            tiled(wide),
            pl.BlockSpec((levels, tile, rank), lambda i: (0, i, 0)),
            whole(two.shape),
        ],
        [near, rows, two],
        flops=6 * rank * points * wide,
        grid=(points // tile,),
        out_specs=[tiled(wide), tiled(len(LATE) * rank), tiled(len(LATE) * rank)],
    )


def chunks(value):
    left, right = value[:, :128], value[:, 128:]
    group = lax.broadcasted_iota(jnp.int32, left.shape, 1) // 32

    def pick(*parts):
        out = parts[3]
        for k in (2, 1, 0):
            out = jnp.where(group == k, parts[k], out)
        return out

    def turn(part, groups):
        return pltpu.roll(part, groups * 32, 1) if groups else part

    even = pick(left, turn(left, 3), turn(right, 2), turn(right, 1))
    odd = pick(turn(left, 3), turn(left, 2), turn(right, 1), right)
    return even, odd


def expand(base, rows_high, rows_low, zero, one, one_more, part, part1, part2, part3):
    def body(
        b_ref, h_ref, l_ref, z_ref, o_ref, m_ref, q0, q1, q2, q3, out, held, even, odd, total
    ):
        _, x, _ = place()
        total[0:128] = z_ref[...]
        total[128:256] = o_ref[...] + m_ref[...]
        for k, ref in ((0, q0), (1, q1)):
            total[pl.ds(pl.multiple_of(256 + ((x ^ k) & 1) * 64, 64), 64)] = ref[:64]
        for k, ref in ((0, q0), (1, q1), (2, q2), (3, q3)):
            base = 64 if k < 2 else 0
            row = pl.multiple_of((x ^ k) * 32, 32)
            total[pl.ds(384 + row, 32)] = ref[base:base + 32]
            total[pl.ds(512 + row, 32)] = ref[base + 32:base + 64]
        left = h_ref[...], l_ref[...]
        value = b_ref[...] + dot3(left, split(total[...]), MATMUL)
        out[...] = value
        held[...] = value
        even[...], odd[...] = chunks(value)

    points, wide = base.shape
    depth = rows_high.shape[1]
    given = [base, rows_high, rows_low, zero, one, one_more, part, part1, part2, part3]
    return call(
        body,
        shapes(base.shape, base.shape, (points, wide // 2), (points, wide // 2)),
        [whole(g.shape) for g in given],
        given,
        [pltpu.VMEM((depth, wide), F32)],
        flops=6 * depth * points * wide,
    )


def gram(left, first, second):
    wide = first.shape[1]
    near = left is first
    tall = left.shape[1]
    part = tall // 4
    given = [first, second] if near else [first, second, left]

    def body(*refs):
        a_ref, b_ref = refs[0], refs[1]
        outs, total = refs[len(given):-1], refs[-1]
        _, x, _ = place()
        mine, beside = split(a_ref[...]), split(b_ref[...])
        if near:
            pairs = (mine, mine), (beside, mine)
        else:
            rows = split(refs[2][...])
            pairs = (rows, mine), (rows, beside)
        for k, (up, down) in enumerate(pairs):
            total[k] = dot3(up, down, ROWS)
        for k, out in enumerate(outs):
            out[...] = total[:, pl.ds(pl.multiple_of((x ^ k) * part, part), part)]

    return call(
        body,
        shapes(*[(2, part, wide)] * 4),
        [whole(g.shape) for g in given],
        given,
        [pltpu.VMEM((2, tall, wide), F32)],
        flops=12 * tall * wide * first.shape[0],
    )


def add_x(near, far_even, far_odd):
    _, rows, wide = near[0].shape
    half = rows // 2

    def body(*refs):
        ins, mine, give = refs[:12], refs[12], refs[13]

        def add(four, block):
            return (four[0][block] + four[1][block]) + (four[2][block] + four[3][block])

        for block in range(2):
            mine[block] = add(ins[:4], block)
        mine[2, :half] = add(ins[4:8], 0)
        mine[2, half:] = add(ins[8:], 0)
        give[:half] = add(ins[4:8], 1)
        give[half:] = add(ins[8:], 1)

    ins = [*near, *far_even, *far_odd]
    return call(body, shapes((3, rows, wide), (rows, wide)), [whole(i.shape) for i in ins], ins)


def cut_y(mine, got):
    blocks, rows, wide = mine.shape

    def body(mine_ref, got_ref, *refs):
        *outs, total = refs
        y, _, _ = place()
        probe = lax.axis_index("probe")
        total[:blocks] = mine_ref[...]
        total[blocks] = got_ref[...]
        for k, out in enumerate(outs):
            out[...] = total[probe ^ y ^ k]

    return call(
        body,
        shapes(*[(rows, wide)] * 4),
        [whole(mine.shape), whole(got.shape)],
        [mine, got],
        [pltpu.VMEM((blocks + 1, rows, wide), F32)],
    )


def cut_z(ins, shift):
    rows, wide = ins[0].shape
    half = rows // 2

    def body(*refs):
        *given, keep, give, total = refs
        _, _, z = place()
        side = (z >> shift) & 1
        total[...] = functools.reduce(jnp.add, [ref[...] for ref in given])
        keep[...] = total[pl.ds(pl.multiple_of(side * half, half), half)]
        give[...] = total[pl.ds(pl.multiple_of((1 - side) * half, half), half)]

    return call(
        body,
        shapes(*[(half, wide)] * 2),
        [whole(i.shape) for i in ins],
        list(ins),
        [pltpu.VMEM((rows, wide), F32)],
    )


def around(parts, scale):
    return [parts[0]] + [swap(parts[k], "leaf", k * scale) for k in (1, 2, 3)]


def near_product(leaf_blocks, block_mask, probes):
    leaf_points = leaf_blocks.shape[1]
    side = block_mask.shape[1]
    span = leaf_points // side

    weights = block_mask[0].astype(F32)
    masked = (
        leaf_blocks.reshape(side, span, side, span) * weights[:, None, :, None]
    ).reshape(leaf_points, leaf_points)
    return jnp.dot(masked, probes, precision=HIGH, preferred_element_type=F32)


def local(leaf_blocks, block_mask, row_factor_stack, column_factor_stack, probes):
    leaf_points = leaf_blocks.shape[1]
    keep, *sent = project_high(column_factor_stack, probes)
    _, one, two, three = around([keep, *sent], 4)
    low0, low1, low2 = project_low(column_factor_stack, probes)
    low2 = low2 + swap(low2, "leaf", 1)
    part3 = two[:64] + three[:64]
    upper = keep + one + two[64:] + three[64:]
    part4 = swap(upper[:32], "leaf", 16)
    five = upper[32:]
    part5 = swap(five, "leaf", 32) + swap(five, "leaf", 48)
    part = jnp.concatenate([part3, part4, part5])
    low2 = low2 + swap(low2, "leaf", 3)
    node2 = swap(low2, "leaf", 4)
    part, blocks, low1 = lax.optimization_barrier((part, leaf_blocks, low1))
    near = near_product(blocks, block_mask, probes)
    part = part + swap(part, "leaf", 1)
    near, low1 = lax.optimization_barrier((near, low1))
    node1 = swap(low1, "leaf", 3)
    part, near = lax.optimization_barrier((part, near))
    part = part + swap(part, "leaf", 3)
    node1, low0 = lax.optimization_barrier((node1, low0))
    node1_more = swap(node1, "leaf", 1)
    node0 = swap(low0, "leaf", 1)
    late = prepare(near, row_factor_stack, node2)
    part, *late = lax.optimization_barrier((part, *late))
    gathered = [swap(part, "leaf", 4), swap(part[64:], "leaf", 8), swap(part[64:], "leaf", 12)]
    result, applied, even, odd = expand(*late, node0, node1, node1_more, part, *gathered)

    even = swap(even, "probe", 2)
    odd = swap(odd, "probe", 2)
    beside = swap(applied, "probe", 1)
    first = around(gram(applied, applied, beside), 4)
    even, *first = lax.optimization_barrier((even, *first))
    second = around(gram(even, applied, beside), 4)
    odd, *second = lax.optimization_barrier((odd, *second))
    third = around(gram(odd, applied, beside), 4)
    mine, give = add_x(first, second, third)
    blocks = around(cut_y(mine, swap(give, "probe", 1)), 16)
    keep, give = cut_z(blocks, 1)
    keep, give = cut_z([keep, swap(give, "leaf", 3)], 0)
    total = keep + swap(give, "leaf", 1)
    return result, total / (leaf_points * lax.axis_size("leaf"))


def solution(mesh):
    return jax.shard_map(
        local,
        mesh=mesh,
        in_specs=(
            P("leaf", None),
            P("leaf", None, None),
            P(None, "leaf", None),
            P(None, "leaf", None),
            P("leaf", "probe"),
        ),
        out_specs=(P("leaf", "probe"), P("leaf", "probe")),
        check_vma=False,
    )
```

```python
import functools

import jax
import jax.numpy as jnp
from jax import lax
from jax.experimental import pallas as pl
from jax.experimental.pallas import tpu as pltpu
from jax.sharding import PartitionSpec as P

HIGH = lax.Precision.HIGH
F32 = jnp.float32
LIMIT = 40 * 2**20
MOST = 53 * 2**20


def swap(value, axis, mask):
    pairs = [(source, source ^ mask) for source in range(lax.axis_size(axis))]
    return lax.ppermute(value, axis, pairs)


def split(value):
    top = value.astype(jnp.bfloat16)
    return top, (value - top.astype(F32)).astype(jnp.bfloat16)


def dot3(left, right, dims):
    dot = functools.partial(
        lax.dot_general, dimension_numbers=(dims, ((), ())), preferred_element_type=F32
    )
    return dot(left[0], right[0]) + (dot(left[0], right[1]) + dot(left[1], right[0]))


ROWS = ((0,), (0,))
MATMUL = ((1,), (0,))


def whole(shape):
    return pl.BlockSpec(shape, lambda *_: (0,) * len(shape))


def shapes(*dims):
    return [jax.ShapeDtypeStruct(d, F32) for d in dims]


def call(
    body, outs, specs, operands, scratch=(), flops=0, grid=(1,), out_specs=None, limit=LIMIT
):
    moved = sum(o.size * 4 for o in operands) + sum(o.size * 4 for o in outs)
    return pl.pallas_call(
        body,
        out_shape=outs,
        grid=grid,
        in_specs=specs,
        out_specs=[whole(o.shape) for o in outs] if out_specs is None else out_specs,
        scratch_shapes=list(scratch),
        compiler_params=pltpu.CompilerParams(vmem_limit_bytes=limit),
        cost_estimate=pl.CostEstimate(flops=flops, bytes_accessed=moved, transcendentals=0),
    )(*operands)


def place():
    leaf = lax.axis_index("leaf")
    return leaf >> 4, (leaf >> 2) & 3, leaf & 3


CUTS = 4


def project(columns, probes, first, outs, emit):
    _, points, rank = columns.shape
    wide = probes.shape[1]
    piece = points // CUTS

    def body(c_hbm, p_hbm, *refs):
        *results, held, given, total, sems = refs
        copies = [
            pltpu.make_async_copy(
                p_hbm.at[pl.ds(i * piece, piece)], given.at[pl.ds(i * piece, piece)], sems.at[0, i]
            )
            for i in range(CUTS)
        ]
        for level in range(3):
            for i in range(CUTS):
                copies.append(
                    pltpu.make_async_copy(
                        c_hbm.at[first + level, pl.ds(i * piece, piece)],
                        held.at[level, pl.ds(i * piece, piece)],
                        sems.at[level + 1, i],
                    )
                )
        for copy in copies:
            copy.start()
        for copy in copies[:CUTS]:
            copy.wait()
        right = split(given[...])
        for level in range(3):
            for copy in copies[(level + 1) * CUTS:(level + 2) * CUTS]:
                copy.wait()
            total[level] = dot3(split(held[level]), right, ROWS)
        emit(total, *results)

    return call(
        body,
        outs,
        [pl.BlockSpec(memory_space=pltpu.HBM)] * 2,
        [columns, probes],
        [
            pltpu.VMEM((3, points, rank), F32),
            pltpu.VMEM((points, wide), F32),
            pltpu.VMEM((3, rank, wide), F32),
            pltpu.SemaphoreType.DMA((4, CUTS)),
        ],
        flops=18 * points * rank * wide,
        limit=MOST,
    )


def project_high(columns, probes):
    def emit(total, keep, one, two, three):
        _, x, _ = place()
        for part, out in ((1, one), (2, two), (3, three)):
            base = 0 if part == 1 else 64
            if part > 1:
                half = ((x ^ part) & 1) * 64
                out[:64] = total[0, pl.ds(pl.multiple_of(half, 64), 64)]
            row = pl.multiple_of((x ^ part) * 32, 32)
            out[base:base + 32] = total[1, pl.ds(row, 32)]
            out[base + 32:base + 64] = total[2, pl.ds(row, 32)]
        row = pl.multiple_of(x * 32, 32)
        keep[:32] = total[1, pl.ds(row, 32)]
        keep[32:] = total[2, pl.ds(row, 32)]

    wide = probes.shape[1]
    outs = shapes((64, wide), (64, wide), (128, wide), (128, wide))
    return project(columns, probes, 3, outs, emit)


def project_low(columns, probes):
    def emit(total, *outs):
        for level, out in enumerate(outs):
            out[...] = total[level]

    outs = shapes(*[(columns.shape[2], probes.shape[1])] * 3)
    return project(columns, probes, 0, outs, emit)


LATE = (0, 1, 3, 4, 5)


def prepare(near, rows, two):
    def body(n_ref, u_ref, t_ref, out, high, low):
        out[...] = n_ref[...] + dot3(split(u_ref[2]), split(t_ref[...]), MATMUL)
        high[...], low[...] = split(jnp.concatenate([u_ref[t] for t in LATE], axis=1))

    levels, points, rank = rows.shape
    wide = near.shape[1]
    tile = 256

    def tiled(width):
        return pl.BlockSpec((tile, width), lambda i: (i, 0))

    late = jax.ShapeDtypeStruct((points, len(LATE) * rank), jnp.bfloat16)
    return call(
        body,
        shapes(near.shape) + [late, late],
        [
            tiled(wide),
            pl.BlockSpec((levels, tile, rank), lambda i: (0, i, 0)),
            whole(two.shape),
        ],
        [near, rows, two],
        flops=6 * rank * points * wide,
        grid=(points // tile,),
        out_specs=[tiled(wide), tiled(len(LATE) * rank), tiled(len(LATE) * rank)],
    )


def chunks(value):
    left, right = value[:, :128], value[:, 128:]
    group = lax.broadcasted_iota(jnp.int32, left.shape, 1) // 32

    def pick(*parts):
        out = parts[3]
        for k in (2, 1, 0):
            out = jnp.where(group == k, parts[k], out)
        return out

    def turn(part, groups):
        return pltpu.roll(part, groups * 32, 1) if groups else part

    even = pick(left, turn(left, 3), turn(right, 2), turn(right, 1))
    odd = pick(turn(left, 3), turn(left, 2), turn(right, 1), right)
    return even, odd


def expand(base, rows_high, rows_low, zero, one, one_more, part, part1, part2, part3):
    def body(
        b_ref, h_ref, l_ref, z_ref, o_ref, m_ref, q0, q1, q3, q2, out, held, even, odd, total
    ):
        _, x, _ = place()
        total[0:128] = z_ref[...]
        total[128:256] = o_ref[...] + m_ref[...]
        for k, ref in ((0, q0), (1, q1)):
            total[pl.ds(pl.multiple_of(256 + ((x ^ k) & 1) * 64, 64), 64)] = ref[:64]
        for k, ref in ((0, q0), (1, q1), (2, q2), (3, q3)):
            base = 64 if k < 2 else 0
            row = pl.multiple_of((x ^ k) * 32, 32)
            total[pl.ds(384 + row, 32)] = ref[base:base + 32]
            total[pl.ds(512 + row, 32)] = ref[base + 32:base + 64]
        left = h_ref[...], l_ref[...]
        value = b_ref[...] + dot3(left, split(total[...]), MATMUL)
        out[...] = value
        held[...] = value
        even[...], odd[...] = chunks(value)

    points, wide = base.shape
    depth = rows_high.shape[1]
    given = [base, rows_high, rows_low, zero, one, one_more, part, part1, part3, part2]
    return call(
        body,
        shapes(base.shape, base.shape, (points, wide // 2), (points, wide // 2)),
        [whole(g.shape) for g in given],
        given,
        [pltpu.VMEM((depth, wide), F32)],
        flops=6 * depth * points * wide,
    )


def gram(left, first, second):
    wide = first.shape[1]
    near = left is first
    tall = left.shape[1]
    part = tall // 4
    given = [first, second] if near else [first, second, left]

    def body(*refs):
        a_ref, b_ref = refs[0], refs[1]
        outs, total = refs[len(given):-1], refs[-1]
        _, x, _ = place()
        mine, beside = split(a_ref[...]), split(b_ref[...])
        if near:
            pairs = (mine, mine), (beside, mine)
        else:
            rows = split(refs[2][...])
            pairs = (rows, mine), (rows, beside)
        for k, (up, down) in enumerate(pairs):
            total[k] = dot3(up, down, ROWS)
        for k, out in enumerate(outs):
            out[...] = total[:, pl.ds(pl.multiple_of((x ^ k) * part, part), part)]

    return call(
        body,
        shapes(*[(2, part, wide)] * 4),
        [whole(g.shape) for g in given],
        given,
        [pltpu.VMEM((2, tall, wide), F32)],
        flops=12 * tall * wide * first.shape[0],
    )


def add_x(near, far_even, far_odd):
    _, rows, wide = near[0].shape
    half = rows // 2

    def body(*refs):
        ins, mine, give = refs[:12], refs[12], refs[13]

        def add(four, block):
            return (four[0][block] + four[1][block]) + (four[2][block] + four[3][block])

        for block in range(2):
            mine[block] = add(ins[:4], block)
        mine[2, :half] = add(ins[4:8], 0)
        mine[2, half:] = add(ins[8:], 0)
        give[:half] = add(ins[4:8], 1)
        give[half:] = add(ins[8:], 1)

    ins = [*near, *far_even, *far_odd]
    return call(body, shapes((3, rows, wide), (rows, wide)), [whole(i.shape) for i in ins], ins)


def cut_y(mine, got):
    blocks, rows, wide = mine.shape

    def body(mine_ref, got_ref, *refs):
        *outs, total = refs
        y, _, _ = place()
        probe = lax.axis_index("probe")
        total[:blocks] = mine_ref[...]
        total[blocks] = got_ref[...]
        for k, out in enumerate(outs):
            out[...] = total[probe ^ y ^ k]

    return call(
        body,
        shapes(*[(rows, wide)] * 4),
        [whole(mine.shape), whole(got.shape)],
        [mine, got],
        [pltpu.VMEM((blocks + 1, rows, wide), F32)],
    )


def cut_z(ins, shift):
    rows, wide = ins[0].shape
    half = rows // 2

    def body(*refs):
        *given, keep, give, total = refs
        _, _, z = place()
        side = (z >> shift) & 1
        total[...] = functools.reduce(jnp.add, [ref[...] for ref in given])
        keep[...] = total[pl.ds(pl.multiple_of(side * half, half), half)]
        give[...] = total[pl.ds(pl.multiple_of((1 - side) * half, half), half)]

    return call(
        body,
        shapes(*[(half, wide)] * 2),
        [whole(i.shape) for i in ins],
        list(ins),
        [pltpu.VMEM((rows, wide), F32)],
    )


def around(parts, scale):
    return [parts[0]] + [swap(parts[k], "leaf", k * scale) for k in (2, 1, 3)]


def near_product(leaf_blocks, block_mask, probes):
    leaf_points = leaf_blocks.shape[1]
    side = block_mask.shape[1]
    span = leaf_points // side

    weights = block_mask[0].astype(F32)
    masked = (
        leaf_blocks.reshape(side, span, side, span) * weights[:, None, :, None]
    ).reshape(leaf_points, leaf_points)
    return jnp.dot(masked, probes, precision=HIGH, preferred_element_type=F32)


def local(leaf_blocks, block_mask, row_factor_stack, column_factor_stack, probes):
    leaf_points = leaf_blocks.shape[1]
    keep, *sent = project_high(column_factor_stack, probes)
    _, two, one, three = around([keep, *sent], 4)
    low0, low1, low2 = project_low(column_factor_stack, probes)
    low2 = low2 + swap(low2, "leaf", 1)
    part3 = two[:64] + three[:64]
    upper = keep + one + two[64:] + three[64:]
    part4 = swap(upper[:32], "leaf", 16)
    five = upper[32:]
    part5 = swap(five, "leaf", 32) + swap(five, "leaf", 48)
    part = jnp.concatenate([part3, part4, part5])
    low2 = low2 + swap(low2, "leaf", 3)
    part, blocks, low1 = lax.optimization_barrier((part, leaf_blocks, low1))
    near = near_product(blocks, block_mask, probes)
    part = part + swap(part, "leaf", 1)
    near, low1 = lax.optimization_barrier((near, low1))
    node1 = swap(low1, "leaf", 3)
    part, near, low2 = lax.optimization_barrier((part, near, low2))
    part = part + swap(part, "leaf", 3)
    node2 = swap(low2, "leaf", 4)
    node1, low0 = lax.optimization_barrier((node1, low0))
    node1_more = swap(node1, "leaf", 1)
    node0 = swap(low0, "leaf", 1)
    part, near, node2 = lax.optimization_barrier((part, near, node2))
    late = prepare(near, row_factor_stack, node2)
    last = swap(part[64:], "leaf", 8)
    gathered = [swap(part, "leaf", 4), last, swap(part[64:], "leaf", 12)]
    result, applied, even, odd = expand(*late, node0, node1, node1_more, part, *gathered)

    beside = swap(applied, "probe", 1)
    even = swap(even, "probe", 2)
    odd = swap(odd, "probe", 2)
    first = around(gram(applied, applied, beside), 4)
    even, *first = lax.optimization_barrier((even, *first))
    second = around(gram(even, applied, beside), 4)
    odd, *second = lax.optimization_barrier((odd, *second))
    third = around(gram(odd, applied, beside), 4)
    mine, give = add_x(first, second, third)
    blocks = around(cut_y(mine, swap(give, "probe", 1)), 16)
    keep, give = cut_z(blocks, 1)
    keep, give = cut_z([keep, swap(give, "leaf", 3)], 0)
    total = keep + swap(give, "leaf", 1)
    return result, total / (leaf_points * lax.axis_size("leaf"))


def solution(mesh):
    return jax.shard_map(
        local,
        mesh=mesh,
        in_specs=(
            P("leaf", None),
            P("leaf", None, None),
            P(None, "leaf", None),
            P(None, "leaf", None),
            P("leaf", "probe"),
        ),
        out_specs=(P("leaf", "probe"), P("leaf", "probe")),
        check_vma=False,
    )
```

```python
import functools

import jax
import jax.numpy as jnp
from jax import lax
from jax.experimental import pallas as pl
from jax.experimental.pallas import tpu as pltpu
from jax.sharding import PartitionSpec as P

HIGH = lax.Precision.HIGH
F32 = jnp.float32
LIMIT = 40 * 2**20
MOST = 53 * 2**20


def swap(value, axis, mask):
    pairs = [(source, source ^ mask) for source in range(lax.axis_size(axis))]
    return lax.ppermute(value, axis, pairs)


def split(value):
    top = value.astype(jnp.bfloat16)
    return top, (value - top.astype(F32)).astype(jnp.bfloat16)


def dot3(left, right, dims):
    dot = functools.partial(
        lax.dot_general, dimension_numbers=(dims, ((), ())), preferred_element_type=F32
    )
    return dot(left[0], right[0]) + (dot(left[0], right[1]) + dot(left[1], right[0]))


ROWS = ((0,), (0,))
MATMUL = ((1,), (0,))


def whole(shape):
    return pl.BlockSpec(shape, lambda *_: (0,) * len(shape))


def shapes(*dims):
    return [jax.ShapeDtypeStruct(d, F32) for d in dims]


def call(
    body, outs, specs, operands, scratch=(), flops=0, grid=(1,), out_specs=None, limit=LIMIT
):
    moved = sum(o.size * 4 for o in operands) + sum(o.size * 4 for o in outs)
    return pl.pallas_call(
        body,
        out_shape=outs,
        grid=grid,
        in_specs=specs,
        out_specs=[whole(o.shape) for o in outs] if out_specs is None else out_specs,
        scratch_shapes=list(scratch),
        compiler_params=pltpu.CompilerParams(vmem_limit_bytes=limit),
        cost_estimate=pl.CostEstimate(flops=flops, bytes_accessed=moved, transcendentals=0),
    )(*operands)


def place():
    leaf = lax.axis_index("leaf")
    return leaf >> 4, (leaf >> 2) & 3, leaf & 3


CUTS = 4


def project(columns, probes, first, outs, emit):
    _, points, rank = columns.shape
    wide = probes.shape[1]
    piece = points // CUTS

    def body(c_hbm, p_hbm, *refs):
        *results, held, given, total, sems = refs
        copies = [
            pltpu.make_async_copy(
                p_hbm.at[pl.ds(i * piece, piece)], given.at[pl.ds(i * piece, piece)], sems.at[0, i]
            )
            for i in range(CUTS)
        ]
        for level in range(3):
            for i in range(CUTS):
                copies.append(
                    pltpu.make_async_copy(
                        c_hbm.at[first + level, pl.ds(i * piece, piece)],
                        held.at[level, pl.ds(i * piece, piece)],
                        sems.at[level + 1, i],
                    )
                )
        for copy in copies:
            copy.start()
        for copy in copies[:CUTS]:
            copy.wait()
        right = split(given[...])
        for level in range(3):
            for copy in copies[(level + 1) * CUTS:(level + 2) * CUTS]:
                copy.wait()
            total[level] = dot3(split(held[level]), right, ROWS)
        emit(total, *results)

    return call(
        body,
        outs,
        [pl.BlockSpec(memory_space=pltpu.HBM)] * 2,
        [columns, probes],
        [
            pltpu.VMEM((3, points, rank), F32),
            pltpu.VMEM((points, wide), F32),
            pltpu.VMEM((3, rank, wide), F32),
            pltpu.SemaphoreType.DMA((4, CUTS)),
        ],
        flops=18 * points * rank * wide,
        limit=MOST,
    )


def project_high(columns, probes):
    def emit(total, keep, one, two, three):
        _, x, _ = place()
        for part, out in ((1, one), (2, two), (3, three)):
            base = 0 if part == 1 else 64
            if part > 1:
                half = ((x ^ part) & 1) * 64
                out[:64] = total[0, pl.ds(pl.multiple_of(half, 64), 64)]
            row = pl.multiple_of((x ^ part) * 32, 32)
            out[base:base + 32] = total[1, pl.ds(row, 32)]
            out[base + 32:base + 64] = total[2, pl.ds(row, 32)]
        row = pl.multiple_of(x * 32, 32)
        keep[:32] = total[1, pl.ds(row, 32)]
        keep[32:] = total[2, pl.ds(row, 32)]

    wide = probes.shape[1]
    outs = shapes((64, wide), (64, wide), (128, wide), (128, wide))
    return project(columns, probes, 3, outs, emit)


def project_low(columns, probes):
    def emit(total, *outs):
        for level, out in enumerate(outs):
            out[...] = total[level]

    outs = shapes(*[(columns.shape[2], probes.shape[1])] * 3)
    return project(columns, probes, 0, outs, emit)


LATE = (0, 1, 3, 4, 5)


def prepare(near, rows, two):
    def body(n_ref, u_ref, t_ref, out, high, low):
        out[...] = n_ref[...] + dot3(split(u_ref[2]), split(t_ref[...]), MATMUL)
        high[...], low[...] = split(jnp.concatenate([u_ref[t] for t in LATE], axis=1))

    levels, points, rank = rows.shape
    wide = near.shape[1]
    tile = 256

    def tiled(width):
        return pl.BlockSpec((tile, width), lambda i: (i, 0))

    late = jax.ShapeDtypeStruct((points, len(LATE) * rank), jnp.bfloat16)
    return call(
        body,
        shapes(near.shape) + [late, late],
        [
            tiled(wide),
            pl.BlockSpec((levels, tile, rank), lambda i: (0, i, 0)),
            whole(two.shape),
        ],
        [near, rows, two],
        flops=6 * rank * points * wide,
        grid=(points // tile,),
        out_specs=[tiled(wide), tiled(len(LATE) * rank), tiled(len(LATE) * rank)],
    )


def chunks(value):
    left, right = value[:, :128], value[:, 128:]
    group = lax.broadcasted_iota(jnp.int32, left.shape, 1) // 32

    def pick(*parts):
        out = parts[3]
        for k in (2, 1, 0):
            out = jnp.where(group == k, parts[k], out)
        return out

    def turn(part, groups):
        return pltpu.roll(part, groups * 32, 1) if groups else part

    even = pick(left, turn(left, 3), turn(right, 2), turn(right, 1))
    odd = pick(turn(left, 3), turn(left, 2), turn(right, 1), right)
    return even, odd


def expand(base, rows_high, rows_low, zero, one, one_more, part, part1, part2, part3):
    def body(
        b_ref, h_ref, l_ref, z_ref, o_ref, m_ref, q0, q1, q3, q2, held, even, odd, total
    ):
        _, x, _ = place()
        total[0:128] = z_ref[...]
        total[128:256] = o_ref[...] + m_ref[...]
        for k, ref in ((0, q0), (1, q1)):
            total[pl.ds(pl.multiple_of(256 + ((x ^ k) & 1) * 64, 64), 64)] = ref[:64]
        for k, ref in ((0, q0), (1, q1), (2, q2), (3, q3)):
            base = 64 if k < 2 else 0
            row = pl.multiple_of((x ^ k) * 32, 32)
            total[pl.ds(384 + row, 32)] = ref[base:base + 32]
            total[pl.ds(512 + row, 32)] = ref[base + 32:base + 64]
        left = h_ref[...], l_ref[...]
        value = b_ref[...] + dot3(left, split(total[...]), MATMUL)
        held[...] = value
        even[...], odd[...] = chunks(value)

    points, wide = base.shape
    depth = rows_high.shape[1]
    given = [base, rows_high, rows_low, zero, one, one_more, part, part1, part3, part2]
    return call(
        body,
        shapes(base.shape, (points, wide // 2), (points, wide // 2)),
        [whole(g.shape) for g in given],
        given,
        [pltpu.VMEM((depth, wide), F32)],
        flops=6 * depth * points * wide,
    )


def gram(left, first, second):
    wide = first.shape[1]
    near = left is first
    tall = left.shape[1]
    part = tall // 4
    given = [first, second] if near else [first, second, left]

    def body(*refs):
        a_ref, b_ref = refs[0], refs[1]
        outs, total = refs[len(given):-1], refs[-1]
        _, x, _ = place()
        mine, beside = split(a_ref[...]), split(b_ref[...])
        if near:
            pairs = (mine, mine), (beside, mine)
        else:
            rows = split(refs[2][...])
            pairs = (rows, mine), (rows, beside)
        for k, (up, down) in enumerate(pairs):
            total[k] = dot3(up, down, ROWS)
        for k, out in enumerate(outs[:4]):
            out[...] = total[:, pl.ds(pl.multiple_of((x ^ k) * part, part), part)]
        if near:
            outs[4][...] = a_ref[...]

    return call(
        body,
        shapes(*[(2, part, wide)] * 4, *[first.shape] * near),
        [whole(g.shape) for g in given],
        given,
        [pltpu.VMEM((2, tall, wide), F32)],
        flops=12 * tall * wide * first.shape[0],
    )


def add_x(near, far_even, far_odd):
    _, rows, wide = near[0].shape
    half = rows // 2

    def body(*refs):
        ins, mine, give = refs[:12], refs[12], refs[13]

        def add(four, block):
            return (four[0][block] + four[1][block]) + (four[2][block] + four[3][block])

        for block in range(2):
            mine[block] = add(ins[:4], block)
        mine[2, :half] = add(ins[4:8], 0)
        mine[2, half:] = add(ins[8:], 0)
        give[:half] = add(ins[4:8], 1)
        give[half:] = add(ins[8:], 1)

    ins = [*near, *far_even, *far_odd]
    return call(body, shapes((3, rows, wide), (rows, wide)), [whole(i.shape) for i in ins], ins)


def cut_y(mine, got):
    blocks, rows, wide = mine.shape

    def body(mine_ref, got_ref, *refs):
        *outs, total = refs
        y, _, _ = place()
        probe = lax.axis_index("probe")
        total[:blocks] = mine_ref[...]
        total[blocks] = got_ref[...]
        for k, out in enumerate(outs):
            out[...] = total[probe ^ y ^ k]

    return call(
        body,
        shapes(*[(rows, wide)] * 4),
        [whole(mine.shape), whole(got.shape)],
        [mine, got],
        [pltpu.VMEM((blocks + 1, rows, wide), F32)],
    )


def cut_z(ins, shift):
    rows, wide = ins[0].shape
    half = rows // 2

    def body(*refs):
        *given, keep, give, total = refs
        _, _, z = place()
        side = (z >> shift) & 1
        total[...] = functools.reduce(jnp.add, [ref[...] for ref in given])
        keep[...] = total[pl.ds(pl.multiple_of(side * half, half), half)]
        give[...] = total[pl.ds(pl.multiple_of((1 - side) * half, half), half)]

    return call(
        body,
        shapes(*[(half, wide)] * 2),
        [whole(i.shape) for i in ins],
        list(ins),
        [pltpu.VMEM((rows, wide), F32)],
    )


def around(parts, scale):
    return [parts[0]] + [swap(parts[k], "leaf", k * scale) for k in (2, 1, 3)]


def near_product(leaf_blocks, block_mask, probes):
    leaf_points = leaf_blocks.shape[1]
    side = block_mask.shape[1]
    span = leaf_points // side

    weights = block_mask[0].astype(F32)
    masked = (
        leaf_blocks.reshape(side, span, side, span) * weights[:, None, :, None]
    ).reshape(leaf_points, leaf_points)
    return jnp.dot(masked, probes, precision=HIGH, preferred_element_type=F32)


def local(leaf_blocks, block_mask, row_factor_stack, column_factor_stack, probes):
    leaf_points = leaf_blocks.shape[1]
    keep, *sent = project_high(column_factor_stack, probes)
    _, two, one, three = around([keep, *sent], 4)
    low0, low1, low2 = project_low(column_factor_stack, probes)
    low2 = low2 + swap(low2, "leaf", 1)
    part3 = two[:64] + three[:64]
    upper = keep + one + two[64:] + three[64:]
    part4 = swap(upper[:32], "leaf", 16)
    five = upper[32:]
    part5 = swap(five, "leaf", 32) + swap(five, "leaf", 48)
    part = jnp.concatenate([part3, part4, part5])
    low2 = low2 + swap(low2, "leaf", 3)
    part, blocks, low1 = lax.optimization_barrier((part, leaf_blocks, low1))
    near = near_product(blocks, block_mask, probes)
    part = part + swap(part, "leaf", 1)
    near, low1 = lax.optimization_barrier((near, low1))
    node1 = swap(low1, "leaf", 3)
    part, near, low2 = lax.optimization_barrier((part, near, low2))
    part = part + swap(part, "leaf", 3)
    node2 = swap(low2, "leaf", 4)
    node1, low0 = lax.optimization_barrier((node1, low0))
    node1_more = swap(node1, "leaf", 1)
    node0 = swap(low0, "leaf", 1)
    part, near, node2 = lax.optimization_barrier((part, near, node2))
    late = prepare(near, row_factor_stack, node2)
    last = swap(part[64:], "leaf", 8)
    gathered = [swap(part, "leaf", 4), last, swap(part[64:], "leaf", 12)]
    applied, even, odd = expand(*late, node0, node1, node1_more, part, *gathered)

    beside = swap(applied, "probe", 1)
    even = swap(even, "probe", 2)
    odd = swap(odd, "probe", 2)
    *first, result = gram(applied, applied, beside)
    first = around(first, 4)
    even, *first = lax.optimization_barrier((even, *first))
    second = around(gram(even, applied, beside), 4)
    odd, *second = lax.optimization_barrier((odd, *second))
    third = around(gram(odd, applied, beside), 4)
    mine, give = add_x(first, second, third)
    blocks = around(cut_y(mine, swap(give, "probe", 1)), 16)
    keep, give = cut_z(blocks, 1)
    keep, give = cut_z([keep, swap(give, "leaf", 3)], 0)
    total = keep + swap(give, "leaf", 1)
    return result, total / (leaf_points * lax.axis_size("leaf"))


def solution(mesh):
    return jax.shard_map(
        local,
        mesh=mesh,
        in_specs=(
            P("leaf", None),
            P("leaf", None, None),
            P(None, "leaf", None),
            P(None, "leaf", None),
            P("leaf", "probe"),
        ),
        out_specs=(P("leaf", "probe"), P("leaf", "probe")),
        check_vma=False,
    )
```

```python
import functools

import jax
import jax.numpy as jnp
from jax import lax
from jax.experimental import pallas as pl
from jax.experimental.pallas import tpu as pltpu
from jax.sharding import PartitionSpec as P

HIGH = lax.Precision.HIGH
F32 = jnp.float32
LIMIT = 40 * 2**20
MOST = 53 * 2**20


def swap(value, axis, mask):
    pairs = [(source, source ^ mask) for source in range(lax.axis_size(axis))]
    return lax.ppermute(value, axis, pairs)


def split(value):
    top = value.astype(jnp.bfloat16)
    return top, (value - top.astype(F32)).astype(jnp.bfloat16)


def dot3(left, right, dims):
    dot = functools.partial(
        lax.dot_general, dimension_numbers=(dims, ((), ())), preferred_element_type=F32
    )
    return dot(left[0], right[0]) + (dot(left[0], right[1]) + dot(left[1], right[0]))


ROWS = ((0,), (0,))
MATMUL = ((1,), (0,))


def whole(shape):
    return pl.BlockSpec(shape, lambda *_: (0,) * len(shape))


def shapes(*dims):
    return [jax.ShapeDtypeStruct(d, F32) for d in dims]


def call(
    body, outs, specs, operands, scratch=(), flops=0, grid=(1,), out_specs=None, limit=LIMIT
):
    moved = sum(o.size * 4 for o in operands) + sum(o.size * 4 for o in outs)
    return pl.pallas_call(
        body,
        out_shape=outs,
        grid=grid,
        in_specs=specs,
        out_specs=[whole(o.shape) for o in outs] if out_specs is None else out_specs,
        scratch_shapes=list(scratch),
        compiler_params=pltpu.CompilerParams(vmem_limit_bytes=limit),
        cost_estimate=pl.CostEstimate(flops=flops, bytes_accessed=moved, transcendentals=0),
    )(*operands)


def place():
    leaf = lax.axis_index("leaf")
    return leaf >> 4, (leaf >> 2) & 3, leaf & 3


CUTS = 8


def project(columns, probes, first, outs, emit):
    _, points, rank = columns.shape
    wide = probes.shape[1]
    piece = points // CUTS

    def body(c_hbm, p_hbm, *refs):
        *results, held, given, total, sems = refs
        copies = [
            pltpu.make_async_copy(
                p_hbm.at[pl.ds(i * piece, piece)], given.at[pl.ds(i * piece, piece)], sems.at[0, i]
            )
            for i in range(CUTS)
        ]
        for level in range(3):
            for i in range(CUTS):
                copies.append(
                    pltpu.make_async_copy(
                        c_hbm.at[first + level, pl.ds(i * piece, piece)],
                        held.at[level, pl.ds(i * piece, piece)],
                        sems.at[level + 1, i],
                    )
                )
        for copy in copies:
            copy.start()
        for copy in copies[:CUTS]:
            copy.wait()
        right = split(given[...])
        for level in range(3):
            for copy in copies[(level + 1) * CUTS:(level + 2) * CUTS]:
                copy.wait()
            total[level] = dot3(split(held[level]), right, ROWS)
        emit(total, *results)

    return call(
        body,
        outs,
        [pl.BlockSpec(memory_space=pltpu.HBM)] * 2,
        [columns, probes],
        [
            pltpu.VMEM((3, points, rank), F32),
            pltpu.VMEM((points, wide), F32),
            pltpu.VMEM((3, rank, wide), F32),
            pltpu.SemaphoreType.DMA((4, CUTS)),
        ],
        flops=18 * points * rank * wide,
        limit=MOST,
    )


def project_high(columns, probes):
    def emit(total, keep, one, two, three):
        _, x, _ = place()
        for part, out in ((1, one), (2, two), (3, three)):
            base = 0 if part == 1 else 64
            if part > 1:
                half = ((x ^ part) & 1) * 64
                out[:64] = total[0, pl.ds(pl.multiple_of(half, 64), 64)]
            row = pl.multiple_of((x ^ part) * 32, 32)
            out[base:base + 32] = total[1, pl.ds(row, 32)]
            out[base + 32:base + 64] = total[2, pl.ds(row, 32)]
        row = pl.multiple_of(x * 32, 32)
        keep[:32] = total[1, pl.ds(row, 32)]
        keep[32:] = total[2, pl.ds(row, 32)]

    wide = probes.shape[1]
    outs = shapes((64, wide), (64, wide), (128, wide), (128, wide))
    return project(columns, probes, 3, outs, emit)


def project_low(columns, probes):
    def emit(total, *outs):
        for level, out in enumerate(outs):
            out[...] = total[level]

    outs = shapes(*[(columns.shape[2], probes.shape[1])] * 3)
    return project(columns, probes, 0, outs, emit)


LATE = (0, 1, 3, 4, 5)


def prepare(near, rows, two):
    def body(n_ref, u_ref, t_ref, out, high, low):
        out[...] = n_ref[...] + dot3(split(u_ref[2]), split(t_ref[...]), MATMUL)
        high[...], low[...] = split(jnp.concatenate([u_ref[t] for t in LATE], axis=1))

    levels, points, rank = rows.shape
    wide = near.shape[1]
    tile = 256

    def tiled(width):
        return pl.BlockSpec((tile, width), lambda i: (i, 0))

    late = jax.ShapeDtypeStruct((points, len(LATE) * rank), jnp.bfloat16)
    return call(
        body,
        shapes(near.shape) + [late, late],
        [
            tiled(wide),
            pl.BlockSpec((levels, tile, rank), lambda i: (0, i, 0)),
            whole(two.shape),
        ],
        [near, rows, two],
        flops=6 * rank * points * wide,
        grid=(points // tile,),
        out_specs=[tiled(wide), tiled(len(LATE) * rank), tiled(len(LATE) * rank)],
    )


def chunks(value):
    left, right = value[:, :128], value[:, 128:]
    group = lax.broadcasted_iota(jnp.int32, left.shape, 1) // 32

    def pick(*parts):
        out = parts[3]
        for k in (2, 1, 0):
            out = jnp.where(group == k, parts[k], out)
        return out

    def turn(part, groups):
        return pltpu.roll(part, groups * 32, 1) if groups else part

    even = pick(left, turn(left, 3), turn(right, 2), turn(right, 1))
    odd = pick(turn(left, 3), turn(left, 2), turn(right, 1), right)
    return even, odd


def expand(base, rows_high, rows_low, zero, one, one_more, part, part1, part2, part3):
    def body(
        b_ref, h_ref, l_ref, z_ref, o_ref, m_ref, q0, q1, q3, q2, held, even, odd, total
    ):
        _, x, _ = place()
        total[0:128] = z_ref[...]
        total[128:256] = o_ref[...] + m_ref[...]
        for k, ref in ((0, q0), (1, q1)):
            total[pl.ds(pl.multiple_of(256 + ((x ^ k) & 1) * 64, 64), 64)] = ref[:64]
        for k, ref in ((0, q0), (1, q1), (2, q2), (3, q3)):
            base = 64 if k < 2 else 0
            row = pl.multiple_of((x ^ k) * 32, 32)
            total[pl.ds(384 + row, 32)] = ref[base:base + 32]
            total[pl.ds(512 + row, 32)] = ref[base + 32:base + 64]
        left = h_ref[...], l_ref[...]
        value = b_ref[...] + dot3(left, split(total[...]), MATMUL)
        held[...] = value
        even[...], odd[...] = chunks(value)

    points, wide = base.shape
    depth = rows_high.shape[1]
    given = [base, rows_high, rows_low, zero, one, one_more, part, part1, part3, part2]
    return call(
        body,
        shapes(base.shape, (points, wide // 2), (points, wide // 2)),
        [whole(g.shape) for g in given],
        given,
        [pltpu.VMEM((depth, wide), F32)],
        flops=6 * depth * points * wide,
    )


def gram(left, first, second):
    wide = first.shape[1]
    near = left is first
    tall = left.shape[1]
    part = tall // 4
    given = [first, second] if near else [first, second, left]

    def body(*refs):
        a_ref, b_ref = refs[0], refs[1]
        outs, total = refs[len(given):-1], refs[-1]
        _, x, _ = place()
        mine, beside = split(a_ref[...]), split(b_ref[...])
        if near:
            pairs = (mine, mine), (beside, mine)
        else:
            rows = split(refs[2][...])
            pairs = (rows, mine), (rows, beside)
        for k, (up, down) in enumerate(pairs):
            total[k] = dot3(up, down, ROWS)
        for k, out in enumerate(outs[:4]):
            out[...] = total[:, pl.ds(pl.multiple_of((x ^ k) * part, part), part)]
        if near:
            outs[4][...] = a_ref[...]

    return call(
        body,
        shapes(*[(2, part, wide)] * 4, *[first.shape] * near),
        [whole(g.shape) for g in given],
        given,
        [pltpu.VMEM((2, tall, wide), F32)],
        flops=12 * tall * wide * first.shape[0],
    )


def add_x(near, far_even, far_odd):
    _, rows, wide = near[0].shape
    half = rows // 2

    def body(*refs):
        ins, mine, give = refs[:12], refs[12], refs[13]

        def add(four, block):
            return (four[0][block] + four[1][block]) + (four[2][block] + four[3][block])

        for block in range(2):
            mine[block] = add(ins[:4], block)
        mine[2, :half] = add(ins[4:8], 0)
        mine[2, half:] = add(ins[8:], 0)
        give[:half] = add(ins[4:8], 1)
        give[half:] = add(ins[8:], 1)

    ins = [*near, *far_even, *far_odd]
    return call(body, shapes((3, rows, wide), (rows, wide)), [whole(i.shape) for i in ins], ins)


def cut_y(mine, got):
    blocks, rows, wide = mine.shape

    def body(mine_ref, got_ref, *refs):
        *outs, total = refs
        y, _, _ = place()
        probe = lax.axis_index("probe")
        total[:blocks] = mine_ref[...]
        total[blocks] = got_ref[...]
        for k, out in enumerate(outs):
            out[...] = total[probe ^ y ^ k]

    return call(
        body,
        shapes(*[(rows, wide)] * 4),
        [whole(mine.shape), whole(got.shape)],
        [mine, got],
        [pltpu.VMEM((blocks + 1, rows, wide), F32)],
    )


def cut_z(ins, shift):
    rows, wide = ins[0].shape
    half = rows // 2

    def body(*refs):
        *given, keep, give, total = refs
        _, _, z = place()
        side = (z >> shift) & 1
        total[...] = functools.reduce(jnp.add, [ref[...] for ref in given])
        keep[...] = total[pl.ds(pl.multiple_of(side * half, half), half)]
        give[...] = total[pl.ds(pl.multiple_of((1 - side) * half, half), half)]

    return call(
        body,
        shapes(*[(half, wide)] * 2),
        [whole(i.shape) for i in ins],
        list(ins),
        [pltpu.VMEM((rows, wide), F32)],
    )


def around(parts, scale):
    return [parts[0]] + [swap(parts[k], "leaf", k * scale) for k in (2, 1, 3)]


def near_product(leaf_blocks, block_mask, probes):
    leaf_points = leaf_blocks.shape[1]
    side = block_mask.shape[1]
    span = leaf_points // side

    weights = block_mask[0].astype(F32)
    masked = (
        leaf_blocks.reshape(side, span, side, span) * weights[:, None, :, None]
    ).reshape(leaf_points, leaf_points)
    return jnp.dot(masked, probes, precision=HIGH, preferred_element_type=F32)


def local(leaf_blocks, block_mask, row_factor_stack, column_factor_stack, probes):
    leaf_points = leaf_blocks.shape[1]
    keep, *sent = project_high(column_factor_stack, probes)
    _, two, one, three = around([keep, *sent], 4)
    low0, low1, low2 = project_low(column_factor_stack, probes)
    low2 = low2 + swap(low2, "leaf", 1)
    part3 = two[:64] + three[:64]
    upper = keep + one + two[64:] + three[64:]
    part4 = swap(upper[:32], "leaf", 16)
    five = upper[32:]
    part5 = swap(five, "leaf", 32) + swap(five, "leaf", 48)
    part = jnp.concatenate([part3, part4, part5])
    low2 = low2 + swap(low2, "leaf", 3)
    part, blocks, low1 = lax.optimization_barrier((part, leaf_blocks, low1))
    near = near_product(blocks, block_mask, probes)
    part = part + swap(part, "leaf", 1)
    near, low1 = lax.optimization_barrier((near, low1))
    node1 = swap(low1, "leaf", 3)
    part, near, low2 = lax.optimization_barrier((part, near, low2))
    part = part + swap(part, "leaf", 3)
    node2 = swap(low2, "leaf", 4)
    node1, low0 = lax.optimization_barrier((node1, low0))
    node1_more = swap(node1, "leaf", 1)
    node0 = swap(low0, "leaf", 1)
    part, near, node2 = lax.optimization_barrier((part, near, node2))
    late = prepare(near, row_factor_stack, node2)
    last = swap(part[64:], "leaf", 8)
    gathered = [swap(part, "leaf", 4), last, swap(part[64:], "leaf", 12)]
    applied, even, odd = expand(*late, node0, node1, node1_more, part, *gathered)

    beside = swap(applied, "probe", 1)
    even = swap(even, "probe", 2)
    odd = swap(odd, "probe", 2)
    *first, result = gram(applied, applied, beside)
    first = around(first, 4)
    even, *first = lax.optimization_barrier((even, *first))
    second = around(gram(even, applied, beside), 4)
    odd, *second = lax.optimization_barrier((odd, *second))
    third = around(gram(odd, applied, beside), 4)
    mine, give = add_x(first, second, third)
    blocks = around(cut_y(mine, swap(give, "probe", 1)), 16)
    keep, give = cut_z(blocks, 1)
    keep, give = cut_z([keep, swap(give, "leaf", 3)], 0)
    total = keep + swap(give, "leaf", 1)
    return result, total / (leaf_points * lax.axis_size("leaf"))


def solution(mesh):
    return jax.shard_map(
        local,
        mesh=mesh,
        in_specs=(
            P("leaf", None),
            P("leaf", None, None),
            P(None, "leaf", None),
            P(None, "leaf", None),
            P("leaf", "probe"),
        ),
        out_specs=(P("leaf", "probe"), P("leaf", "probe")),
        check_vma=False,
    )
```
